256 devices in a mesh: blk: 128 (over y, z, x_lo, core), bank: 2 (over x_hi).
Axes of the slice: x: 4 (x_hi: 2, x_lo: 2; x = x_hi * 2 + x_lo), y: 4, z: 8, core: 2. Of those that a mesh axis runs over, the one named last changes fastest.
Arguments:
- tile_pool: bfloat16 [512, 256, 256], P('blk'), may hold values from -600 to 600
- tile_list: int32 [256], P('blk'), may hold values from 0 to 3, as said below
- counts: int32 [128], replicated, may hold values from 0 to 2, as said below
- projections: bfloat16 [512, 192, 192], P(('blk', 'bank')), may hold values from -600 to 600
Outputs:
- peak_map: float32 [256, 256, 256], P('blk', 'bank')
- zscore_map: float32 [256, 256, 256], P('blk', 'bank')
The draws below stay inside these ranges and needn't reach their ends.
Inputs may be any that keep to these rules, and one draw needn't show every extreme that they name: `tile_list`: the 2 entries of one owner are distinct. `counts`: owners 2k and 2k + 1 together hold exactly 2 live slots, and owner 2k holds at least 1 of them.
All inputs are finite; a program needn't handle non-finite values.
Results may differ from the reference program's by a relative error of at most 0.008.
Values may be sent and summed in bfloat16 or wider, within the bound.
A program may use at most 64 MiB of HBM per device.

```python
import math
import jax
import jax.numpy as jnp
from jax import lax

TILE = 256
PSIZE = 192
CAP = 2
PROJ = 2
STEPS = 4
OWNERS = 128
BANKS = 2
POOL = 4
TILES_ALL = 256
POOL_ALL = 512
PROJ_ALL = 512
ORIENTS = 16


def scale_field(key, count, edge):
    subkeys = jax.random.split(key, 2)
    row_scale = jnp.exp(jax.random.uniform(subkeys[0], (count, edge, 1)) * math.log(10.0))
    col_scale = jnp.exp(jax.random.uniform(subkeys[1], (count, 1, edge)) * math.log(10.0))
    return row_scale * col_scale


def draw_tile_pool(key, part):
    key = jax.random.fold_in(key, 11)
    subkeys = jax.random.split(key, 2)
    shape = (POOL_ALL, TILE, TILE)
    base_field = jnp.clip(jax.random.normal(subkeys[0], shape), -6.0, 6.0)
    return (base_field * scale_field(subkeys[1], POOL_ALL, TILE)).astype(jnp.bfloat16)


def draw_projections(key, part):
    key = jax.random.fold_in(key, 12)
    subkeys = jax.random.split(key, 2)
    shape = (PROJ_ALL, PSIZE, PSIZE)
    base_field = jnp.clip(jax.random.normal(subkeys[0], shape), -6.0, 6.0)
    return (base_field * scale_field(subkeys[1], PROJ_ALL, PSIZE)).astype(jnp.bfloat16)


def draw_tile_list(key, part):
    key = jax.random.fold_in(key, 13)
    owner_total = TILES_ALL // CAP
    subkeys = jax.random.split(key, owner_total)
    orders = jax.vmap(lambda subkey: jax.random.permutation(subkey, POOL))(subkeys)
    return orders[:, :CAP].reshape(-1).astype(jnp.int32)


def draw_counts(key, part):
    key = jax.random.fold_in(key, 14)
    subkeys = jax.random.split(key, 2)
    pair_total = TILES_ALL // CAP // 2
    surplus = jax.random.randint(subkeys[0], (pair_total,), 0, CAP // 2 + 1)
    forced = jax.random.randint(subkeys[1], (), 0, pair_total)
    surplus = jnp.where(jnp.arange(pair_total) == forced, CAP // 2, surplus)
    return jnp.stack([CAP // 2 + surplus, CAP // 2 - surplus], axis=1).reshape(-1).astype(jnp.int32)


def setup_inputs(seed: int = 0) -> dict:
    arg_keys = jax.random.split(jax.random.key(seed), 5)
    tile_pool = draw_tile_pool(jax.random.fold_in(arg_keys[4], 71), 0)
    tile_list = draw_tile_list(jax.random.fold_in(arg_keys[4], 71), 0)
    counts = draw_counts(jax.random.fold_in(arg_keys[4], 71), 0)
    projections = draw_projections(jax.random.fold_in(arg_keys[4], 71), 0)
    return {"tile_pool": tile_pool, "tile_list": tile_list, "counts": counts, "projections": projections}


def make_tables(edge_len):
    indices = jnp.arange(edge_len, dtype=jnp.int32)
    phase_index = indices[:, None] * indices[None, :] % edge_len
    phase_angle = phase_index.astype(jnp.float32) * (2.0 * math.pi / edge_len)
    cosine = jnp.cos(phase_angle).astype(jnp.bfloat16)
    sine = jnp.sin(phase_angle).astype(jnp.bfloat16)
    forward_cols = jnp.concatenate([cosine, -sine], axis=1)
    stack_rows = jnp.concatenate([cosine, sine], axis=0)
    inverse_rows = jnp.concatenate([cosine, -sine], axis=0)
    return (forward_cols, stack_rows, inverse_rows)

def spectrum(fields, tables):
    forward_cols, stack_rows, inverse_rows = tables
    edge_len = fields.shape[-1]
    row_pass = jnp.einsum('bij,jk->bik', fields.astype(jnp.float32), forward_cols.astype(jnp.float32)).astype(jnp.bfloat16)
    products = jnp.einsum('ij,bjk->bik', stack_rows.astype(jnp.float32), row_pass.astype(jnp.float32))
    real_part = products[:, :edge_len, :edge_len] + products[:, edge_len:, edge_len:]
    imag_part = products[:, :edge_len, edge_len:] - products[:, edge_len:, :edge_len]
    return jnp.concatenate([real_part, imag_part], axis=-1)

def unit_tiles(tiles):
    as_float = tiles.astype(jnp.float32)
    centre = lax.optimization_barrier(jnp.mean(as_float, axis=(-2, -1), keepdims=True))
    centred = as_float - centre
    mean_square = lax.optimization_barrier(jnp.mean(centred * centred, axis=(-2, -1), keepdims=True))
    return (centred / jnp.sqrt(mean_square + 1e-05)).astype(jnp.bfloat16)

def unit_projections(images, edge_len):
    as_float = images.astype(jnp.float32)
    side = images.shape[-1]
    centre = lax.optimization_barrier(jnp.mean(as_float, axis=(-2, -1), keepdims=True))
    centred = as_float - centre
    mean_square = lax.optimization_barrier(jnp.mean(centred * centred, axis=(-2, -1), keepdims=True))
    unit_image = (centred / (side * jnp.sqrt(mean_square + 1e-05))).astype(jnp.bfloat16)
    return jnp.pad(unit_image, ((0, 0), (0, edge_len - side), (0, edge_len - side)))

def correlate(tile_spec, proj_spectra, tables):
    forward_cols, stack_rows, inverse_rows = tables
    edge_len = tile_spec.shape[0]
    tile_real = tile_spec[None, :, :edge_len].astype(jnp.float32)
    tile_imag = tile_spec[None, :, edge_len:].astype(jnp.float32)
    proj_real = proj_spectra[:, :, :edge_len].astype(jnp.float32)
    proj_imag = proj_spectra[:, :, edge_len:].astype(jnp.float32)
    cross_spec = jnp.concatenate([tile_real * proj_real + tile_imag * proj_imag, tile_imag * proj_real - tile_real * proj_imag], axis=-1).astype(jnp.bfloat16)
    products = jnp.einsum('ij,bjk->bik', stack_rows.astype(jnp.float32), cross_spec.astype(jnp.float32))
    inner_pass = jnp.concatenate([products[:, :edge_len, :edge_len] - products[:, edge_len:, edge_len:], products[:, edge_len:, :edge_len] + products[:, :edge_len, edge_len:]], axis=-1).astype(jnp.bfloat16)
    return jnp.einsum('bij,jk->bik', inner_pass.astype(jnp.float32), inverse_rows.astype(jnp.float32)) * (1.0 / edge_len)

def reference(tile_pool, tile_list, counts, projections):
    tables = make_tables(TILE)
    padded = unit_projections(projections, TILE)
    grouped = padded.reshape(PROJ_ALL // PROJ, PROJ, TILE, TILE)
    spectra = lax.map(lambda group_fields: spectrum(group_fields, tables).astype(jnp.bfloat16), grouped)
    slot_ids = jnp.arange(TILES_ALL, dtype=jnp.int32)
    live_slot = slot_ids % CAP < counts[slot_ids // CAP]
    live_order = jnp.nonzero(live_slot, size=TILES_ALL // 2)[0].astype(jnp.int32)

    def one_slot(slot_id):
        owner_index = slot_id // CAP
        tile_row = owner_index * POOL + tile_list[slot_id]
        unit_tile = unit_tiles(lax.dynamic_slice_in_dim(tile_pool, tile_row, 1, 0))
        tile_spec = (spectrum(unit_tile, tables) * (1.0 / TILE)).astype(jnp.bfloat16)[0]
        steps_ahead = jnp.arange(STEPS, dtype=jnp.int32)
        bank_half = jnp.arange(BANKS, dtype=jnp.int32)
        blocks = (((owner_index - steps_ahead) % OWNERS)[:, None] * BANKS + bank_half[None, :]).reshape(-1)
        chosen = spectra[blocks].reshape(ORIENTS, TILE, 2 * TILE)
        correlation = correlate(tile_spec, chosen, tables)
        best_map = lax.optimization_barrier(jnp.max(correlation, axis=0))
        total_map = lax.optimization_barrier(jnp.sum(correlation, axis=0))
        squares = lax.optimization_barrier(jnp.sum(correlation * correlation, axis=0))
        mean_map = total_map / ORIENTS
        spread_map = jnp.maximum(squares / ORIENTS - mean_map * mean_map, 0.3)
        return (best_map, (best_map - mean_map) / jnp.sqrt(spread_map))
    peak_rows, score_rows = lax.map(one_slot, live_order)
    peak_map = jnp.zeros((TILES_ALL, TILE, TILE), jnp.float32).at[live_order].set(peak_rows)
    zscore_map = jnp.zeros((TILES_ALL, TILE, TILE), jnp.float32).at[live_order].set(score_rows)
    return (peak_map, zscore_map)
```

```python
import functools

import jax
import jax.numpy as jnp
import ml_dtypes
import numpy as np
from jax import lax
from jax.experimental import pallas as pl
from jax.experimental.pallas import tpu as pltpu
from jax.sharding import PartitionSpec as P

EDGE = 256
SIDE = 192
HALF = 128
CHIPS = 64
UNIT = (288, 128)
BF16 = jnp.bfloat16
F32 = jnp.float32
MESH = pl.DeviceIdType.MESH
STAGE = 16


def slot(block, bank, r):
    return (block * 2 + bank) * 2 + r


def make_tables():
    index = np.arange(EDGE)
    angle = (index[:, None] * index[None, :] % EDGE) * (2.0 * np.pi / EDGE)
    cosine = np.cos(angle)
    sine = np.sin(angle)
    alternate = 1.0 - 2.0 * (index % 2)
    row_pass = np.concatenate([cosine[:, :HALF], -sine[:, :HALF]], axis=1)
    row_pass[:, HALF] = alternate
    first = np.zeros((EDGE, EDGE))
    first[:SIDE] = row_pass[:SIDE]
    second = np.zeros((EDGE, EDGE))
    second[:HALF] = row_pass[:HALF]
    second[SIDE:] = row_pass[HALF:SIDE]
    rows = np.stack([row_pass, first, second])
    tile_cols = np.block([[cosine, sine], [-sine, cosine]])
    proj_cols = np.block(
        [[cosine[:, :SIDE], sine[:, :SIDE]], [-sine[:, :SIDE], cosine[:, :SIDE]]]
    )
    back_cols = np.stack(
        [
            np.block(
                [
                    [cosine[part : part + HALF], -sine[part : part + HALF]],
                    [sine[part : part + HALF], cosine[part : part + HALF]],
                ]
            )
            for part in (0, HALF)
        ]
    )
    back_rows = np.concatenate([2.0 * cosine[:HALF], -2.0 * sine[:HALF]], axis=0)
    back_rows[0] = 1.0
    back_rows[HALF] = alternate
    back_rows /= EDGE
    cast = lambda table: table.astype(np.float32).astype(ml_dtypes.bfloat16)
    alt_rows = np.broadcast_to(alternate, (16, EDGE))
    flip_rows = np.eye(HALF)[::-1]
    return tuple(cast(t) for t in (rows, tile_cols, proj_cols, back_cols, back_rows, alt_rows, flip_rows))


def dot(a, b):
    return jnp.dot(a, b, preferred_element_type=F32)


def kernel(
    pool, tile_list, counts, raw, rows, tile_cols, proj_cols, back_cols, back_rows, alt_rows, flip_rows,
    peak_out, score_out,
    buf, back, spec_re, spec_im, circ, stats, send_sem, recv_sem, load_sem,
):
    me = lax.axis_index("blk")
    bank = lax.axis_index("bank")
    chip = me // 2
    core = me % 2
    odd = chip % 2
    other = 1 - bank

    def device(ahead, which, side):
        return (((chip + ahead + CHIPS) % CHIPS) * 2 + which, side)

    load = pltpu.make_async_copy(back_cols.at[bank], back, load_sem)
    load.start()
    barrier = pltpu.get_barrier_semaphore()

    def greet(target):
        pl.semaphore_signal(barrier, inc=1, device_id=target, device_id_type=MESH)

    greet(device(0, 1 - core, bank))
    greet(device(0, 0, other))

    @pl.when(core == 1)
    def _():
        greet(device(0, 1, other))

    @pl.when(odd == 0)
    def _():
        greet(device(1, core, bank))
        greet(device(1, core, other))

        @pl.when(core == 0)
        def _():
            greet(device(-2, 1, bank))

    @pl.when(odd == 1)
    def _():
        for side in (bank, other):
            for which in (0, 1):
                greet(device(-1, which, side))
        for which in (0, 1):
            greet(device(-2, which, bank))

    for r in range(2):
        image = raw[r].astype(F32)
        centred = image - jnp.sum(image) * (1.0 / (SIDE * SIDE))
        power = jnp.sum(centred * centred) * (1.0 / (SIDE * SIDE))
        unit = centred / (SIDE * jnp.sqrt(power + 1e-5))
        right = jnp.concatenate([unit[:96, HALF:], unit[96:, HALF:]], axis=1)
        packed = jnp.concatenate([unit[:, :HALF], right], axis=0).astype(BF16)

        @pl.when(core == 0)
        def _():
            buf[slot(0, 0, r)] = packed

        @pl.when(core == 1)
        def _():
            buf[slot(1, 0, r)] = packed

    @pl.when((odd == 1) & (core == 1))
    def _():
        pl.semaphore_wait(barrier, 6)

    @pl.when((odd == 0) | (core == 0))
    def _():
        pl.semaphore_wait(barrier, 7)

    def gather(core, odd):
        sends = []

        def send(source, target, to):
            copy = pltpu.make_async_remote_copy(
                src_ref=buf.at[source],
                dst_ref=buf.at[target],
                send_sem=send_sem.at[len(sends)],
                recv_sem=recv_sem.at[target],
                device_id=to,
                device_id_type=MESH,
            )
            copy.start()
            sends.append(copy)

        def arrive(target):
            pltpu.make_async_remote_copy(
                src_ref=buf.at[target],
                dst_ref=buf.at[target],
                send_sem=send_sem.at[0],
                recv_sem=recv_sem.at[target],
                device_id=device(0, 1 - core, bank),
                device_id_type=MESH,
            ).wait_recv()

        def share(at):
            send(at, at, device(0, 1 - core, bank))

        own = [slot(core, 0, r) for r in range(2)]
        sides = ((0, bank), (1, other))
        if odd:
            for r in range(2):
                target = slot(1, 0, 0) if core == 1 and r == 0 else STAGE + 1 - core
                send(own[r], target, device(2, r, bank))
        elif core == 1:
            for r in range(2):
                send(own[r], slot(1, 0, r), device(2, 0, bank))
        for r in range(2):
            send(own[r], slot(core, 1, r), device(0, 1 if core == 1 else r, other))
        if not odd:
            for r in range(2):
                for at, side in sides:
                    send(own[r], slot(2 + core, at, r), device(1, r, side))
        if core == 0:
            for r in range(2):
                send(own[r], own[r], device(0, 1, bank))
        if odd:
            for which in (1, 0):
                at = slot(1, 0, 0) if which == 1 and core == 0 else STAGE + 1 - which
                arrive(at)
                for to, side in sides:
                    send(at, slot(2 + which, to, core), device(-1, core, side))
                if which == 1 and core == 1:
                    send(at, slot(1, 0, 1), device(0, 0, bank))
        if core == 1:
            for r in range(2):
                arrive(slot(1, 1, r))
                send(slot(1, 1, r), slot(1, 1, r), device(2, 0, bank))
        arrive(slot(0, 1, core))
        share(slot(0, 1, core))
        for block in (3, 2):
            for at in range(2):
                arrive(slot(block, at, core))
                share(slot(block, at, core))
        if core == 1:
            for r in range(2):
                arrive(slot(0, 0, r))
        arrive(slot(0, 1, 1 - core))
        for block in (3, 2):
            for at in range(2):
                arrive(slot(block, at, 1 - core))
        if core == 0:
            for r in range(2):
                if not (odd and r == 0):
                    arrive(slot(1, 0, r))
            for r in range(2):
                arrive(slot(1, 1, r))
        for copy in sends:
            copy.wait_send()

    for which in (0, 1):
        for parity in (0, 1):
            pl.when((core == which) & (odd == parity))(functools.partial(gather, which, parity))

    lane = lax.broadcasted_iota(jnp.int32, (1, EDGE), 1)
    is_edge = (lane % HALF) == 0

    res, ims = [], []
    for s in range(2):
        image = pool[tile_list[s]].astype(F32)
        centred = image - jnp.sum(image) * (1.0 / (EDGE * EDGE))
        power = jnp.sum(centred * centred) * (1.0 / (EDGE * EDGE))
        unit = (centred / jnp.sqrt(power + 1e-5)).astype(BF16)
        passed = dot(unit, rows[0])
        res.append(passed[:, :HALF])
        ims.append(passed[:, HALF:])
        column = lax.dot_general(
            alt_rows[...], unit, (((1,), (1,)), ((), ())), preferred_element_type=F32
        )
        column = column[:8]
        swapped = jnp.concatenate([column[:, HALF:], column[:, :HALF]], axis=1)
        column = jnp.where(bank == 1, swapped, column)
        spread = jnp.broadcast_to(column[:1], (HALF, EDGE))
        spread = pltpu.roll(spread, HALF + 1, 1, stride=1, stride_axis=0)
        circ[s] = dot(flip_rows[...], spread[:, :SIDE].astype(BF16)).astype(BF16)
    tile_re = jnp.concatenate(res, axis=1).astype(BF16)
    tile_im = jnp.where(is_edge, 0.0, jnp.concatenate(ims, axis=1)).astype(BF16)
    products = dot(tile_cols[...], jnp.concatenate([tile_re, tile_im], axis=0)) * (1.0 / EDGE)
    for s in range(2):
        part = products[:, s * HALF : (s + 1) * HALF].astype(BF16).astype(F32)
        double = jnp.concatenate([part, part], axis=1)
        spec_re[s] = double[:EDGE]
        spec_im[s] = double[EDGE:]

    stats[:, 0] = jnp.full((2, HALF, EDGE), -1e30, F32)
    stats[:, 1:] = jnp.zeros((2, 2, HALF, EDGE), F32)

    def block_step(block, carry):
        parts_re, parts_im = [], []
        for r in range(2):
            unit = buf[block * 2 + r]
            right = unit[SIDE:]
            top = dot(jnp.concatenate([unit[:96], right], axis=1), rows[1])
            bottom = dot(jnp.concatenate([unit[96:SIDE], right], axis=1), rows[2])
            passed = jnp.concatenate([top, bottom], axis=0)
            parts_re.append(passed[:, :HALF])
            parts_im.append(passed[:, HALF:])
        row_re = jnp.concatenate(parts_re, axis=1).astype(BF16)
        row_im = jnp.concatenate(parts_im, axis=1)
        row_edge = jnp.where(is_edge, row_im, 0.0).astype(BF16)
        row_im = jnp.where(is_edge, 0.0, row_im).astype(BF16)
        products = dot(proj_cols[...], jnp.concatenate([row_re, row_im], axis=0))
        proj_re = products[:EDGE].astype(BF16).astype(F32)
        proj_im = products[EDGE:].astype(BF16).astype(F32)
        for s in range(2):
            cross_re = spec_re[s] * proj_re + spec_im[s] * proj_im
            cross_im = spec_im[s] * proj_re - spec_re[s] * proj_im
            cross = jnp.concatenate([cross_re.astype(BF16), cross_im.astype(BF16)], axis=0)
            inner = dot(back[...], cross)
            inner_re = inner[:HALF].astype(BF16)
            inner_im = (inner[HALF:] + dot(circ[s], row_edge)).astype(BF16)
            stacked = jnp.concatenate(
                [
                    jnp.concatenate([inner_re[:, :HALF], inner_im[:, :HALF]], axis=1),
                    jnp.concatenate([inner_re[:, HALF:], inner_im[:, HALF:]], axis=1),
                ],
                axis=0,
            )
            corr = dot(stacked, back_rows[...])
            one, two = corr[:HALF], corr[HALF:]
            stats[s, 0] = jnp.maximum(stats[s, 0], jnp.maximum(one, two))
            stats[s, 1] = stats[s, 1] + (one + two)
            stats[s, 2] = stats[s, 2] + (one * one + two * two)
        return carry

    load.wait()
    lax.fori_loop(0, 8, block_step, 0)

    live = counts[me]
    for s in range(2):
        keep = s < live
        peak = stats[s, 0]
        mean = stats[s, 1] * (1.0 / 16)
        variance = jnp.maximum(stats[s, 2] * (1.0 / 16) - mean * mean, 0.3)
        peak_out[s] = jnp.where(keep, peak, 0.0)
        score_out[s] = jnp.where(keep, (peak - mean) / jnp.sqrt(variance), 0.0)


def body(tile_pool, tile_list, counts, projections):
    tables = make_tables()
    rows, tile_cols, proj_cols, back_cols, back_rows, alt_rows, flip_rows = [jnp.asarray(t) for t in tables]
    vmem = pl.BlockSpec(memory_space=pltpu.VMEM)
    smem = pl.BlockSpec(memory_space=pltpu.SMEM)
    out = jax.ShapeDtypeStruct((2, HALF, EDGE), F32)
    return pl.pallas_call(
        kernel,
        out_shape=(out, out),
        in_specs=[vmem, smem, smem] + [vmem] * 4
        + [pl.BlockSpec(memory_space=pl.ANY), vmem, vmem, vmem],
        out_specs=(vmem, vmem),
        scratch_shapes=[
            pltpu.VMEM((STAGE + 2,) + UNIT, BF16),
            pltpu.VMEM((EDGE, 2 * EDGE), BF16),
            pltpu.VMEM((2, EDGE, EDGE), F32),
            pltpu.VMEM((2, EDGE, EDGE), F32),
            pltpu.VMEM((2, HALF, SIDE), BF16),
            pltpu.VMEM((2, 3, HALF, EDGE), F32),
            pltpu.SemaphoreType.DMA((24,)),
            pltpu.SemaphoreType.DMA((STAGE + 2,)),
            pltpu.SemaphoreType.DMA,
        ],
        compiler_params=pltpu.CompilerParams(
            collective_id=0, has_side_effects=True, vmem_limit_bytes=48 << 20
        ),
    )(tile_pool, tile_list, counts, projections, rows, tile_cols, proj_cols, back_cols, back_rows, alt_rows, flip_rows)


def solution(mesh):
    in_specs = (P("blk", None, None), P("blk"), P(), P(("blk", "bank"), None, None))
    out_specs = (P("blk", "bank", None), P("blk", "bank", None))
    return jax.shard_map(body, mesh=mesh, in_specs=in_specs, out_specs=out_specs, check_vma=False)
```

```python
import functools

import jax
import jax.numpy as jnp
import ml_dtypes
import numpy as np
from jax import lax
from jax.experimental import pallas as pl
from jax.experimental.pallas import tpu as pltpu
from jax.sharding import PartitionSpec as P

EDGE = 256
SIDE = 192
HALF = 128
CHIPS = 64
UNIT = (288, 128)
BF16 = jnp.bfloat16
F32 = jnp.float32
MESH = pl.DeviceIdType.MESH
STAGE = 10


def slot(block, at):
    return block * 2 + at


def make_tables():
    index = np.arange(EDGE)
    angle = (index[:, None] * index[None, :] % EDGE) * (2.0 * np.pi / EDGE)
    cosine = np.cos(angle)
    sine = np.sin(angle)
    alternate = 1.0 - 2.0 * (index % 2)
    row_pass = np.concatenate([cosine[:, :HALF], -sine[:, :HALF]], axis=1)
    row_pass[:, HALF] = alternate
    first = np.zeros((EDGE, EDGE))
    first[:SIDE] = row_pass[:SIDE]
    second = np.zeros((EDGE, EDGE))
    second[:HALF] = row_pass[:HALF]
    second[SIDE:] = row_pass[HALF:SIDE]
    rows = np.stack([row_pass, first, second])
    tile_cols = np.block([[cosine, sine], [-sine, cosine]])
    proj_cols = np.block(
        [[cosine[:, :SIDE], sine[:, :SIDE]], [-sine[:, :SIDE], cosine[:, :SIDE]]]
    )
    back_cols = np.stack(
        [
            np.block(
                [
                    [cosine[part : part + HALF], -sine[part : part + HALF]],
                    [sine[part : part + HALF], cosine[part : part + HALF]],
                ]
            )
            for part in (0, HALF)
        ]
    )
    back_rows = np.concatenate([2.0 * cosine[:HALF], -2.0 * sine[:HALF]], axis=0)
    back_rows[0] = 1.0
    back_rows[HALF] = alternate
    back_rows /= EDGE
    cast = lambda table: table.astype(np.float32).astype(ml_dtypes.bfloat16)
    alt_rows = np.broadcast_to(alternate, (16, EDGE))
    flip_rows = np.eye(HALF)[::-1]
    return tuple(cast(t) for t in (rows, tile_cols, proj_cols, back_cols, back_rows, alt_rows, flip_rows))


def dot(a, b):
    return jnp.dot(a, b, preferred_element_type=F32)


def kernel(
    pool_in, tile_list, counts, raw_in, rows_in, tile_cols_in, proj_cols_in, back_cols_in,
    back_rows_in, alt_in, flip_in,
    peak_out, score_out,
    pool, raw, rows, tile_cols, proj_cols, back, back_rows, alt_rows, flip_rows,
    mine, buf, chosen, landed, spec, circ, stats, parts, taken,
    load_sem, send_sem, recv_sem, tile_send, tile_recv, part_send, part_recv,
):
    me = lax.axis_index("blk")
    bank = lax.axis_index("bank")
    chip = me // 2
    core = me % 2
    odd = chip % 2
    other = 1 - bank

    def device(ahead, which, side):
        return (((chip + ahead + CHIPS) % CHIPS) * 2 + which, side)

    sibling = device(0, 1 - core, bank)
    sources = (
        raw_in, pool_in, rows_in, alt_in, flip_in, tile_cols_in, proj_cols_in,
        back_cols_in.at[bank], back_rows_in,
    )
    targets = (raw, pool, rows, alt_rows, flip_rows, tile_cols, proj_cols, back, back_rows)
    loads = [
        pltpu.make_async_copy(source, target, load_sem.at[n])
        for n, (source, target) in enumerate(zip(sources, targets))
    ]
    for load in loads:
        load.start()

    barrier = pltpu.get_barrier_semaphore()

    def greet(target):
        pl.semaphore_signal(barrier, inc=1, device_id=target, device_id_type=MESH)

    greet(sibling)
    greet(device(0, 0, other))
    greet(device(0, 1, other))
    greet(device(-2, 1, bank))

    @pl.when(odd == 0)
    def _():
        greet(device(1, core, bank))
        greet(device(1, core, other))

    @pl.when((odd == 1) | (core == 0))
    def _():
        greet(device(-2, 0, bank))

    @pl.when(odd == 1)
    def _():
        for side in (bank, other):
            for which in (0, 1):
                greet(device(-1, which, side))

    loads[0].wait()
    for r in range(2):
        image = raw[r].astype(F32)
        centred = image - jnp.sum(image) * (1.0 / (SIDE * SIDE))
        power = jnp.sum(centred * centred) * (1.0 / (SIDE * SIDE))
        unit = centred / (SIDE * jnp.sqrt(power + 1e-5))
        right = jnp.concatenate([unit[:96, HALF:], unit[96:, HALF:]], axis=1)
        packed = jnp.concatenate([unit[:, :HALF], right], axis=0).astype(BF16)
        mine[r] = packed

        @pl.when(core == r)
        def _():
            buf[slot(r, 0)] = packed

    loads[1].wait()
    for s in range(2):
        chosen[s] = pool[tile_list[s]]

    @pl.when(odd == 1)
    def _():
        pl.semaphore_wait(barrier, 7)

    @pl.when((odd == 0) & (core == 0))
    def _():
        pl.semaphore_wait(barrier, 8)

    @pl.when((odd == 0) & (core == 1))
    def _():
        pl.semaphore_wait(barrier, 9)

    variants = [(which, parity) for which in (0, 1) for parity in (0, 1)]
    sent = {variant: 0 for variant in variants}

    def copy_of(source, target, index, to):
        return pltpu.make_async_remote_copy(
            src_ref=source,
            dst_ref=buf.at[target],
            send_sem=send_sem.at[index],
            recv_sem=recv_sem.at[target],
            device_id=to,
            device_id_type=MESH,
        )

    def send(variant, source, target, to):
        copy_of(source, target, sent[variant], to).start()
        sent[variant] += 1

    def arrive(target):
        copy_of(buf.at[target], target, 0, sibling).wait_recv()

    def each_variant(phase):
        for variant in variants:
            here = (core == variant[0]) & (odd == variant[1])
            pl.when(here)(functools.partial(phase, variant))

    sides = ((0, bank), (1, other))

    def first(variant):
        core, odd = variant
        if odd:
            for r in range(2):
                target = slot(4, 0) if core == 1 else STAGE
                send(variant, mine.at[r], target, device(2, r, bank))
        elif core == 1:
            for r in range(2):
                send(variant, mine.at[r], slot(4, 0), device(2, r, bank))
        send(variant, mine.at[1 - core], slot(core, 0), device(0, 1 - core, bank))
        for r in range(2):
            send(variant, mine.at[r], slot(core, 1), device(0, r, other))
        if not odd:
            for r in range(2):
                for at, side in sides:
                    send(variant, mine.at[r], slot(2 + core, at), device(1, r, side))

    def pass_on(variant):
        core, odd = variant
        if odd:
            for block, at in ((3, slot(4, 0)), (2, STAGE)):
                arrive(at)
                for to, side in sides:
                    send(variant, buf.at[at], slot(block, to), device(-1, core, side))
        arrive(slot(1, 1))
        send(variant, buf.at[slot(1, 1)], slot(4, 1), device(2, core, bank))

    def finish(variant):
        for index in range(sent[variant]):
            copy_of(mine.at[0], 0, index, sibling).wait_send()

    each_variant(first)
    tile_copies = [
        pltpu.make_async_remote_copy(
            src_ref=chosen.at[s],
            dst_ref=landed.at[s],
            send_sem=tile_send.at[s],
            recv_sem=tile_recv.at[s],
            device_id=sibling,
            device_id_type=MESH,
        )
        for s in range(2)
    ]
    for copy in tile_copies:
        copy.start()

    lane = lax.broadcasted_iota(jnp.int32, (1, EDGE), 1)
    is_edge = (lane % HALF) == 0
    is_guest = counts[2 * chip] == 2
    is_first = core == 0

    stats[:, 0] = jnp.full((2, HALF, EDGE), -1e30, F32)
    stats[:, 1:] = jnp.zeros((2, 2, HALF, EDGE), F32)

    for load in loads[2:6]:
        load.wait()
    for copy in tile_copies:
        copy.wait_recv()
    here = [chosen[s].astype(F32) for s in range(2)]
    there = [landed[s].astype(F32) for s in range(2)]
    images = (
        jnp.where(is_first, here[0], there[0]),
        jnp.where(
            is_guest,
            jnp.where(is_first, here[1], there[1]),
            jnp.where(is_first, there[0], here[0]),
        ),
    )
    res, ims = [], []
    for s in range(2):
        image = images[s]
        centred = image - jnp.sum(image) * (1.0 / (EDGE * EDGE))
        power = jnp.sum(centred * centred) * (1.0 / (EDGE * EDGE))
        unit = (centred / jnp.sqrt(power + 1e-5)).astype(BF16)
        passed = dot(unit, rows[0])
        res.append(passed[:, :HALF])
        ims.append(passed[:, HALF:])
        column = lax.dot_general(
            alt_rows[...], unit, (((1,), (1,)), ((), ())), preferred_element_type=F32
        )[:8]
        swapped = jnp.concatenate([column[:, HALF:], column[:, :HALF]], axis=1)
        column = jnp.where(bank == 1, swapped, column)
        spread = jnp.broadcast_to(column[:1], (HALF, EDGE))
        spread = pltpu.roll(spread, HALF + 1, 1, stride=1, stride_axis=0)
        circ[s] = dot(flip_rows[...], spread[:, :SIDE].astype(BF16)).astype(BF16)
    tile_re = jnp.concatenate(res, axis=1).astype(BF16)
    tile_im = jnp.where(is_edge, 0.0, jnp.concatenate(ims, axis=1)).astype(BF16)
    products = dot(tile_cols[...], jnp.concatenate([tile_re, tile_im], axis=0)) * (1.0 / EDGE)
    for s in range(2):
        part = products[:, s * HALF : (s + 1) * HALF].astype(BF16)
        spec[s] = jnp.concatenate([part, part], axis=1)

    for load in loads[6:]:
        load.wait()
    each_variant(pass_on)

    def row_stage(block):
        parts_re, parts_im = [], []
        for at in range(2):
            unit = buf[slot(block, at)]
            right = unit[SIDE:]
            top = dot(jnp.concatenate([unit[:96], right], axis=1), rows[1])
            bottom = dot(jnp.concatenate([unit[96:SIDE], right], axis=1), rows[2])
            passed = jnp.concatenate([top, bottom], axis=0)
            parts_re.append(passed[:, :HALF])
            parts_im.append(passed[:, HALF:])
        row_re = jnp.concatenate(parts_re, axis=1).astype(BF16)
        row_im = jnp.concatenate(parts_im, axis=1)
        edge = jnp.where(is_edge, row_im, 0.0).astype(BF16)
        row_im = jnp.where(is_edge, 0.0, row_im).astype(BF16)
        return jnp.concatenate([row_re, row_im], axis=0), edge

    def spectra(blocks):
        passed = [row_stage(block) for block in blocks]
        return [(dot(proj_cols[...], row).astype(BF16), edge) for row, edge in passed]

    def cross_stage(s, proj):
        proj_re, proj_im = proj[:EDGE].astype(F32), proj[EDGE:].astype(F32)
        tile_re, tile_im = spec[s, :EDGE].astype(F32), spec[s, EDGE:].astype(F32)
        cross_re = (tile_re * proj_re + tile_im * proj_im).astype(BF16)
        cross_im = (tile_im * proj_re - tile_re * proj_im).astype(BF16)
        return jnp.concatenate([cross_re, cross_im], axis=0)

    def correlate(pairs):
        crosses = [cross_stage(s, proj) for s, (proj, _) in pairs]
        inners = [dot(back[...], cross) for cross in crosses]
        extras = [dot(circ[s], edge) for s, (_, edge) in pairs]
        corrs = []
        for inner, extra in zip(inners, extras):
            inner_re = inner[:HALF].astype(BF16)
            inner_im = (inner[HALF:] + extra).astype(BF16)
            stacked = [
                jnp.concatenate([inner_re[:, lanes], inner_im[:, lanes]], axis=1)
                for lanes in (slice(0, HALF), slice(HALF, EDGE))
            ]
            corrs.append(dot(jnp.concatenate(stacked, axis=0), back_rows[...]))
        for (s, _), corr in zip(pairs, corrs):
            one, two = corr[:HALF], corr[HALF:]
            stats[s, 0] = jnp.maximum(stats[s, 0], jnp.maximum(one, two))
            stats[s, 1] = stats[s, 1] + (one + two)
            stats[s, 2] = stats[s, 2] + (one * one + two * two)

    arrive(slot(1 - core, 0))
    arrive(slot(0, 1))
    now, spare = spectra((0, 1))
    correlate([(0, now), (1, now)])
    arrive_edge = spare[1]

    @pl.when(odd == 0)
    def _():
        arrive(slot(4, 0))

    arrive(slot(4, 1))
    (far,) = spectra((4,))
    chosen_far = (
        jnp.where(is_guest, far[0].astype(F32), spare[0].astype(F32)).astype(BF16),
        jnp.where(is_guest, far[1].astype(F32), arrive_edge.astype(F32)).astype(BF16),
    )
    correlate([(0, far), (1, chosen_far)])
    for block in (3, 2):
        for at in range(2):
            arrive(slot(block, at))
    one, two = spectra((3, 2))
    correlate([(0, one), (0, two), (1, one), (1, two)])

    parts[...] = stats[...].astype(BF16)
    meet = pltpu.make_async_remote_copy(
        src_ref=parts,
        dst_ref=taken,
        send_sem=part_send,
        recv_sem=part_recv,
        device_id=sibling,
        device_id_type=MESH,
    )
    meet.start()
    each_variant(finish)
    for copy in tile_copies:
        copy.wait_send()
    meet.wait_recv()
    peaks, scores = [], []
    for s in range(2):
        peak = jnp.maximum(stats[s, 0], taken[s, 0].astype(F32))
        mean = (stats[s, 1] + taken[s, 1].astype(F32)) * (1.0 / 16)
        square = (stats[s, 2] + taken[s, 2].astype(F32)) * (1.0 / 16)
        variance = jnp.maximum(square - mean * mean, 0.3)
        peaks.append(peak)
        scores.append((peak - mean) / jnp.sqrt(variance))
    live = counts[me]
    for out, maps in ((peak_out, peaks), (score_out, scores)):
        out[0] = jnp.where(live > 0, jnp.where(is_first, maps[0], maps[1]), 0.0)
        out[1] = jnp.where(live > 1, maps[1], 0.0)
    meet.wait_send()


def body(tile_pool, tile_list, counts, projections):
    tables = [jnp.asarray(t) for t in make_tables()]
    any_spec = pl.BlockSpec(memory_space=pl.ANY)
    vmem = pl.BlockSpec(memory_space=pltpu.VMEM)
    smem = pl.BlockSpec(memory_space=pltpu.SMEM)
    out = jax.ShapeDtypeStruct((2, HALF, EDGE), F32)
    return pl.pallas_call(
        kernel,
        out_shape=(out, out),
        in_specs=[any_spec, smem, smem] + [any_spec] * 8,
        out_specs=(vmem, vmem),
        scratch_shapes=[
            pltpu.VMEM((4, EDGE, EDGE), BF16),
            pltpu.VMEM((2, SIDE, SIDE), BF16),
            pltpu.VMEM((3, EDGE, EDGE), BF16),
            pltpu.VMEM((2 * EDGE, 2 * EDGE), BF16),
            pltpu.VMEM((2 * EDGE, 2 * SIDE), BF16),
            pltpu.VMEM((EDGE, 2 * EDGE), BF16),
            pltpu.VMEM((EDGE, EDGE), BF16),
            pltpu.VMEM((16, EDGE), BF16),
            pltpu.VMEM((HALF, HALF), BF16),
            pltpu.VMEM((2,) + UNIT, BF16),
            pltpu.VMEM((STAGE + 1,) + UNIT, BF16),
            pltpu.VMEM((2, EDGE, EDGE), BF16),
            pltpu.VMEM((2, EDGE, EDGE), BF16),
            pltpu.VMEM((2, 2 * EDGE, EDGE), BF16),
            pltpu.VMEM((2, HALF, SIDE), BF16),
            pltpu.VMEM((2, 3, HALF, EDGE), F32),
            pltpu.VMEM((2, 3, HALF, EDGE), BF16),
            pltpu.VMEM((2, 3, HALF, EDGE), BF16),
            pltpu.SemaphoreType.DMA((9,)),
            pltpu.SemaphoreType.DMA((20,)),
            pltpu.SemaphoreType.DMA((STAGE + 1,)),
            pltpu.SemaphoreType.DMA((2,)),
            pltpu.SemaphoreType.DMA((2,)),
            pltpu.SemaphoreType.DMA,
            pltpu.SemaphoreType.DMA,
        ],
        compiler_params=pltpu.CompilerParams(
            collective_id=0, has_side_effects=True, vmem_limit_bytes=56 << 20
        ),
    )(tile_pool, tile_list, counts, projections, *tables)


def solution(mesh):
    in_specs = (P("blk", None, None), P("blk"), P(), P(("blk", "bank"), None, None))
    out_specs = (P("blk", "bank", None), P("blk", "bank", None))
    return jax.shard_map(body, mesh=mesh, in_specs=in_specs, out_specs=out_specs, check_vma=False)
```

```python
import functools

import jax
import jax.numpy as jnp
import ml_dtypes
import numpy as np
from jax import lax
from jax.experimental import pallas as pl
from jax.experimental.pallas import tpu as pltpu
from jax.sharding import PartitionSpec as P

EDGE = 256
SIDE = 192
HALF = 128
CHIPS = 64
UNIT = (288, 128)
PIECE = 144
BF16 = jnp.bfloat16
F32 = jnp.float32
MESH = pl.DeviceIdType.MESH
STAGE = 10


def slot(block, at):
    return block * 2 + at


def make_tables():
    index = np.arange(EDGE)
    angle = (index[:, None] * index[None, :] % EDGE) * (2.0 * np.pi / EDGE)
    cosine = np.cos(angle)
    sine = np.sin(angle)
    alternate = 1.0 - 2.0 * (index % 2)
    row_pass = np.concatenate([cosine[:, :HALF], -sine[:, :HALF]], axis=1)
    row_pass[:, HALF] = alternate
    first = np.zeros((EDGE, EDGE))
    first[:SIDE] = row_pass[:SIDE]
    second = np.zeros((EDGE, EDGE))
    second[:HALF] = row_pass[:HALF]
    second[SIDE:] = row_pass[HALF:SIDE]
    rows = np.stack([row_pass, first, second])
    tile_cols = np.block([[cosine, sine], [-sine, cosine]])
    proj_cols = np.block(
        [[cosine[:, :SIDE], sine[:, :SIDE]], [-sine[:, :SIDE], cosine[:, :SIDE]]]
    )
    back_cols = np.stack(
        [
            np.block(
                [
                    [cosine[part : part + HALF], -sine[part : part + HALF]],
                    [sine[part : part + HALF], cosine[part : part + HALF]],
                ]
            )
            for part in (0, HALF)
        ]
    )
    back_rows = np.concatenate([2.0 * cosine[:HALF], -2.0 * sine[:HALF]], axis=0)
    back_rows[0] = 1.0
    back_rows[HALF] = alternate
    back_rows /= EDGE
    cast = lambda table: table.astype(np.float32).astype(ml_dtypes.bfloat16)
    alt_rows = np.broadcast_to(alternate, (16, EDGE))
    flip_rows = np.eye(HALF)[::-1]
    return tuple(cast(t) for t in (rows, tile_cols, proj_cols, back_cols, back_rows, alt_rows, flip_rows))


def dot(a, b):
    return jnp.dot(a, b, preferred_element_type=F32)


def kernel(
    pool_in, tile_list, counts, raw_in, rows_in, tile_cols_in, proj_cols_in, back_cols_in,
    back_rows_in, alt_in, flip_in,
    own_out, taken_out,
    pool, raw, rows, tile_cols, proj_cols, back, back_rows, alt_rows, flip_rows,
    mine, buf, chosen, landed, spec, circ, stats, held_proj, held_edge, parts,
    load_sem, send_sem, recv_sem, half_recv, tile_send, tile_recv, part_send, part_recv,
):
    me = lax.axis_index("blk")
    bank = lax.axis_index("bank")
    chip = me // 2
    core = me % 2
    odd = chip % 2
    first_plane = (chip // 2) % 8 == 0
    other = 1 - bank

    def device(ahead, which, side):
        return (((chip + ahead + CHIPS) % CHIPS) * 2 + which, side)

    sibling = device(0, 1 - core, bank)
    sources = (
        raw_in, pool_in, rows_in, alt_in, flip_in, tile_cols_in, proj_cols_in,
        back_cols_in.at[bank], back_rows_in,
    )
    targets = (raw, pool, rows, alt_rows, flip_rows, tile_cols, proj_cols, back, back_rows)
    loads = [
        pltpu.make_async_copy(source, target, load_sem.at[n])
        for n, (source, target) in enumerate(zip(sources, targets))
    ]
    loads[0].start()

    barrier = pltpu.get_barrier_semaphore()

    def greet(target):
        pl.semaphore_signal(barrier, inc=1, device_id=target, device_id_type=MESH)

    greet(sibling)
    greet(device(0, 0, other))
    greet(device(0, 1, other))
    greet(device(-2, 1, bank))

    @pl.when(odd == 0)
    def _():
        greet(device(1, core, bank))
        greet(device(1, core, other))

    @pl.when((odd == 1) | (core == 0))
    def _():
        greet(device(-2, 0, bank))

    @pl.when(odd == 1)
    def _():
        for side in (bank, other):
            for which in (0, 1):
                greet(device(-1, which, side))

    loads[0].wait()
    for load in loads[1:]:
        load.start()
    packs = []
    for r in range(2):
        image = raw[r].astype(F32)
        centred = image - jnp.sum(image) * (1.0 / (SIDE * SIDE))
        power = jnp.sum(centred * centred) * (1.0 / (SIDE * SIDE))
        unit = centred / (SIDE * jnp.sqrt(power + 1e-5))
        right = jnp.concatenate([unit[:96, HALF:], unit[96:, HALF:]], axis=1)
        packs.append(jnp.concatenate([unit[:, :HALF], right], axis=0))
    for r in range(2):
        mine[r] = packs[r].astype(BF16)
    buf[2 * core] = jnp.where(core == 0, packs[0], packs[1]).astype(BF16)

    @pl.when(odd == 1)
    def _():
        pl.semaphore_wait(barrier, 7)

    @pl.when((odd == 0) & (core == 0))
    def _():
        pl.semaphore_wait(barrier, 8)

    @pl.when((odd == 0) & (core == 1))
    def _():
        pl.semaphore_wait(barrier, 9)

    variants = [(which, parity) for which in (0, 1) for parity in (0, 1)]
    sent = {variant: [] for variant in variants}

    def copy_of(source, target, sent_sem, got_sem, to):
        return pltpu.make_async_remote_copy(
            src_ref=source,
            dst_ref=target,
            send_sem=sent_sem,
            recv_sem=got_sem,
            device_id=to,
            device_id_type=MESH,
        )

    def send(variant, source, target, to):
        index = len(sent[variant])
        sent[variant].append(UNIT[0])
        copy_of(source, buf.at[target], send_sem.at[index], recv_sem.at[target], to).start()

    def send_piece(variant, source, piece, target, got_sem, to):
        index = len(sent[variant])
        sent[variant].append(PIECE)
        rows_of = pl.ds(piece * PIECE, PIECE)
        copy_of(
            source.at[rows_of], buf.at[target, rows_of], send_sem.at[index], got_sem, to
        ).start()

    def arrive(target):
        copy_of(buf.at[target], buf.at[target], send_sem.at[0], recv_sem.at[target], sibling).wait_recv()

    def each_variant(phase, when=True):
        for variant in variants:
            here = (core == variant[0]) & (odd == variant[1]) & when
            pl.when(here)(functools.partial(phase, variant))

    sides = ((0, bank), (1, other))

    def first(variant):
        core, odd = variant
        if odd:
            target = slot(4, 0) if core == 1 else STAGE
            for piece in range(2):
                for r in range(2):
                    got = half_recv.at[2 * (1 - core) + piece]
                    send_piece(variant, mine.at[r], piece, target, got, device(2, r, bank))
        elif core == 1:
            for r in range(2):
                send(variant, mine.at[r], slot(4, 0), device(2, r, bank))
        send(variant, mine.at[1 - core], slot(core, 0), device(0, 1 - core, bank))
        for r in range(2):
            send(variant, mine.at[r], slot(core, 1), device(0, r, other))
        if not odd:
            for r in range(2):
                for at, side in sides:
                    send(variant, mine.at[r], slot(2 + core, at), device(1, r, side))

    def pass_far(variant):
        core, odd = variant
        arrive(slot(1, 1))
        send(variant, buf.at[slot(1, 1)], slot(4, 1), device(2, core, bank))

    def pass_near(variant):
        core, odd = variant
        if odd:
            for piece in range(2):
                for n, (block, at) in enumerate(((3, slot(4, 0)), (2, STAGE))):
                    rows_of = pl.ds(piece * PIECE, PIECE)
                    place = buf.at[at, rows_of]
                    got = half_recv.at[2 * n + piece]
                    copy_of(place, place, send_sem.at[0], got, sibling).wait_recv()
                    for to, side in sides:
                        target = slot(block, to)
                        send_piece(
                            variant, buf.at[at], piece, target, recv_sem.at[target],
                            device(-1, core, side),
                        )

    def finish(variant):
        for index, size in enumerate(sent[variant]):
            piece = mine.at[0, pl.ds(0, size)]
            copy_of(piece, piece, send_sem.at[index], recv_sem.at[0], sibling).wait_send()

    each_variant(first)
    loads[1].wait()
    for s in range(2):
        chosen[s] = pool[tile_list[s]]
    tile_copies = [
        pltpu.make_async_remote_copy(
            src_ref=chosen.at[s],
            dst_ref=landed.at[s],
            send_sem=tile_send.at[s],
            recv_sem=tile_recv.at[s],
            device_id=sibling,
            device_id_type=MESH,
        )
        for s in range(2)
    ]
    for copy in tile_copies:
        copy.start()

    lane = lax.broadcasted_iota(jnp.int32, (1, EDGE), 1)
    is_edge = (lane % HALF) == 0
    is_guest = counts[2 * chip] == 2
    is_first = core == 0

    stats[:, 0] = jnp.full((2, HALF, EDGE), -1e30, F32)
    stats[:, 1:] = jnp.zeros((2, 2, HALF, EDGE), F32)

    for load in loads[2:6]:
        load.wait()
    for copy in tile_copies:
        copy.wait_recv()
    here = [chosen[s].astype(F32) for s in range(2)]
    there = [landed[s].astype(F32) for s in range(2)]
    images = (
        jnp.where(is_first, here[0], there[0]),
        jnp.where(
            is_guest,
            jnp.where(is_first, here[1], there[1]),
            jnp.where(is_first, there[0], here[0]),
        ),
    )
    res, ims = [], []
    for s in range(2):
        image = images[s]
        centred = image - jnp.sum(image) * (1.0 / (EDGE * EDGE))
        power = jnp.sum(centred * centred) * (1.0 / (EDGE * EDGE))
        unit = (centred / jnp.sqrt(power + 1e-5)).astype(BF16)
        passed = dot(unit, rows[0])
        res.append(passed[:, :HALF])
        ims.append(passed[:, HALF:])
        column = lax.dot_general(
            alt_rows[...], unit, (((1,), (1,)), ((), ())), preferred_element_type=F32
        )[:8]
        swapped = jnp.concatenate([column[:, HALF:], column[:, :HALF]], axis=1)
        column = jnp.where(bank == 1, swapped, column)
        spread = jnp.broadcast_to(column[:1], (HALF, EDGE))
        spread = pltpu.roll(spread, HALF + 1, 1, stride=1, stride_axis=0)
        circ[s] = dot(flip_rows[...], spread[:, :SIDE].astype(BF16)).astype(BF16)
    tile_re = jnp.concatenate(res, axis=1).astype(BF16)
    tile_im = jnp.where(is_edge, 0.0, jnp.concatenate(ims, axis=1)).astype(BF16)
    products = dot(tile_cols[...], jnp.concatenate([tile_re, tile_im], axis=0)) * (1.0 / EDGE)
    for s in range(2):
        part = products[:, s * HALF : (s + 1) * HALF].astype(BF16)
        spec[s] = jnp.concatenate([part, part], axis=1)

    for load in loads[6:]:
        load.wait()
    before = {variant: list(sizes) for variant, sizes in sent.items()}
    each_variant(pass_near, jnp.logical_not(first_plane))
    each_variant(pass_far)
    after = dict(sent)
    sent.update(before)

    def row_stage(block):
        parts_re, parts_im = [], []
        for at in range(2):
            unit = buf[slot(block, at)]
            right = unit[SIDE:]
            top = dot(jnp.concatenate([unit[:96], right], axis=1), rows[1])
            bottom = dot(jnp.concatenate([unit[96:SIDE], right], axis=1), rows[2])
            passed = jnp.concatenate([top, bottom], axis=0)
            parts_re.append(passed[:, :HALF])
            parts_im.append(passed[:, HALF:])
        row_re = jnp.concatenate(parts_re, axis=1).astype(BF16)
        row_im = jnp.concatenate(parts_im, axis=1)
        edge = jnp.where(is_edge, row_im, 0.0).astype(BF16)
        row_im = jnp.where(is_edge, 0.0, row_im).astype(BF16)
        return jnp.concatenate([row_re, row_im], axis=0), edge

    def spectra(blocks):
        passed = [row_stage(block) for block in blocks]
        return [(dot(proj_cols[...], row).astype(BF16), edge) for row, edge in passed]

    def cross_stage(s, proj):
        proj_re, proj_im = proj[:EDGE].astype(F32), proj[EDGE:].astype(F32)
        tile_re, tile_im = spec[s, :EDGE].astype(F32), spec[s, EDGE:].astype(F32)
        cross_re = (tile_re * proj_re + tile_im * proj_im).astype(BF16)
        cross_im = (tile_im * proj_re - tile_re * proj_im).astype(BF16)
        return jnp.concatenate([cross_re, cross_im], axis=0)

    def correlate(pairs):
        crosses = [cross_stage(s, proj) for s, (proj, _) in pairs]
        inners = [dot(back[...], cross) for cross in crosses]
        extras = [dot(circ[s], edge) for s, (_, edge) in pairs]
        corrs = []
        for inner, extra in zip(inners, extras):
            inner_re = inner[:HALF].astype(BF16)
            inner_im = (inner[HALF:] + extra).astype(BF16)
            stacked = [
                jnp.concatenate([inner_re[:, lanes], inner_im[:, lanes]], axis=1)
                for lanes in (slice(0, HALF), slice(HALF, EDGE))
            ]
            corrs.append(dot(jnp.concatenate(stacked, axis=0), back_rows[...]))
        for (s, _), corr in zip(pairs, corrs):
            one, two = corr[:HALF], corr[HALF:]
            stats[s, 0] = jnp.maximum(stats[s, 0], jnp.maximum(one, two))
            stats[s, 1] = stats[s, 1] + (one + two)
            stats[s, 2] = stats[s, 2] + (one * one + two * two)

    arrive(slot(1 - core, 0))
    arrive(slot(0, 1))
    now, spare = spectra((0, 1))
    correlate([(0, now), (1, now)])

    def chip_before():
        for block in (3, 2):
            for at in range(2):
                arrive(slot(block, at))
        one, two = spectra((3, 2))
        correlate([(0, one), (0, two), (1, one), (1, two)])

    def two_before():
        @pl.when(odd == 0)
        def _():
            arrive(slot(4, 0))

        arrive(slot(4, 1))
        (far,) = spectra((4,))
        guest = [jnp.where(is_guest, f.astype(F32), c.astype(F32)).astype(BF16) for f, c in zip(far, held())]
        correlate([(0, far), (1, guest)])

    held_proj[...], held_edge[...] = spare

    def held():
        return held_proj[...], held_edge[...]

    each_variant(pass_near, first_plane)
    sent.update(after)

    def last_steps(step, carry):
        pl.when((step == 0) == (odd == 1))(chip_before)
        pl.when((step == 0) == (odd == 0))(two_before)
        return carry

    lax.fori_loop(0, 2, last_steps, 0)

    moves = []
    for s in range(2):
        parts[s] = stats[s].astype(BF16)
        moves.append(
            copy_of(parts.at[s], taken_out.at[s], part_send.at[s], part_recv.at[s], sibling)
        )
        moves.append(pltpu.make_async_copy(parts.at[s], own_out.at[s], load_sem.at[s]))
        moves[-2].start()
        moves[-1].start()
    each_variant(finish)
    for copy in tile_copies:
        copy.wait_send()
    for move in moves:
        move.wait()


def merge_kernel(counts, own, taken, peak_out, score_out):
    me = lax.axis_index("blk")
    is_first = me % 2 == 0
    live = counts[me]
    peaks, scores = [], []
    for s in range(2):
        mine, theirs = own[s].astype(F32), taken[s].astype(F32)
        peak = jnp.maximum(mine[0], theirs[0])
        mean = (mine[1] + theirs[1]) * (1.0 / 16)
        square = (mine[2] + theirs[2]) * (1.0 / 16)
        variance = jnp.maximum(square - mean * mean, 0.3)
        peaks.append(peak)
        scores.append((peak - mean) / jnp.sqrt(variance))
    for out, maps in ((peak_out, peaks), (score_out, scores)):
        out[0] = jnp.where(live > 0, jnp.where(is_first, maps[0], maps[1]), 0.0)
        out[1] = jnp.where(live > 1, maps[1], 0.0)


def body(tile_pool, tile_list, counts, projections):
    tables = [jnp.asarray(t) for t in make_tables()]
    any_spec = pl.BlockSpec(memory_space=pl.ANY)
    vmem = pl.BlockSpec(memory_space=pltpu.VMEM)
    smem = pl.BlockSpec(memory_space=pltpu.SMEM)
    own, taken = pl.pallas_call(
        kernel,
        out_shape=(
            jax.ShapeDtypeStruct((2, 3, HALF, EDGE), BF16),
            jax.ShapeDtypeStruct((2, 3, HALF, EDGE), BF16),
        ),
        in_specs=[any_spec, smem, smem] + [any_spec] * 8,
        out_specs=(any_spec, any_spec),
        scratch_shapes=[
            pltpu.VMEM((4, EDGE, EDGE), BF16),
            pltpu.VMEM((2, SIDE, SIDE), BF16),
            pltpu.VMEM((3, EDGE, EDGE), BF16),
            pltpu.VMEM((2 * EDGE, 2 * EDGE), BF16),
            pltpu.VMEM((2 * EDGE, 2 * SIDE), BF16),
            pltpu.VMEM((EDGE, 2 * EDGE), BF16),
            pltpu.VMEM((EDGE, EDGE), BF16),
            pltpu.VMEM((16, EDGE), BF16),
            pltpu.VMEM((HALF, HALF), BF16),
            pltpu.VMEM((2,) + UNIT, BF16),
            pltpu.VMEM((STAGE + 1,) + UNIT, BF16),
            pltpu.VMEM((2, EDGE, EDGE), BF16),
            pltpu.VMEM((2, EDGE, EDGE), BF16),
            pltpu.VMEM((2, 2 * EDGE, EDGE), BF16),
            pltpu.VMEM((2, HALF, SIDE), BF16),
            pltpu.VMEM((2, 3, HALF, EDGE), F32),
            pltpu.VMEM((2 * EDGE, EDGE), BF16),
            pltpu.VMEM((SIDE, EDGE), BF16),
            pltpu.VMEM((2, 3, HALF, EDGE), BF16),
            pltpu.SemaphoreType.DMA((9,)),
            pltpu.SemaphoreType.DMA((20,)),
            pltpu.SemaphoreType.DMA((STAGE + 1,)),
            pltpu.SemaphoreType.DMA((4,)),
            pltpu.SemaphoreType.DMA((2,)),
            pltpu.SemaphoreType.DMA((2,)),
            pltpu.SemaphoreType.DMA((2,)),
            pltpu.SemaphoreType.DMA((2,)),
        ],
        compiler_params=pltpu.CompilerParams(
            collective_id=0, has_side_effects=True, vmem_limit_bytes=56 << 20
        ),
    )(tile_pool, tile_list, counts, projections, *tables)
    out = jax.ShapeDtypeStruct((2, HALF, EDGE), F32)
    part = pl.BlockSpec((2, 3, HALF // 2, EDGE), lambda i: (0, 0, i, 0))
    out_part = pl.BlockSpec((2, HALF // 2, EDGE), lambda i: (0, i, 0))
    return pl.pallas_call(
        merge_kernel,
        grid=(2,),
        out_shape=(out, out),
        in_specs=[smem, part, part],
        out_specs=(out_part, out_part),
    )(counts, own, taken)


def solution(mesh):
    in_specs = (P("blk", None, None), P("blk"), P(), P(("blk", "bank"), None, None))
    out_specs = (P("blk", "bank", None), P("blk", "bank", None))
    return jax.shard_map(body, mesh=mesh, in_specs=in_specs, out_specs=out_specs, check_vma=False)
```

```python
import functools

import jax
import jax.numpy as jnp
import ml_dtypes
import numpy as np
from jax import lax
from jax.experimental import pallas as pl
from jax.experimental.pallas import tpu as pltpu
from jax.sharding import PartitionSpec as P

EDGE = 256
SIDE = 192
HALF = 128
CHIPS = 64
UNIT = (288, 128)
PIECE = 144
BF16 = jnp.bfloat16
F32 = jnp.float32
MESH = pl.DeviceIdType.MESH
STAGE = 10


def slot(block, at):
    return block * 2 + at


def make_tables():
    index = np.arange(EDGE)
    angle = (index[:, None] * index[None, :] % EDGE) * (2.0 * np.pi / EDGE)
    cosine = np.cos(angle)
    sine = np.sin(angle)
    alternate = 1.0 - 2.0 * (index % 2)
    row_pass = np.concatenate([cosine[:, :HALF], -sine[:, :HALF]], axis=1)
    row_pass[:, HALF] = alternate
    first = np.zeros((EDGE, EDGE))
    first[:SIDE] = row_pass[:SIDE]
    second = np.zeros((EDGE, EDGE))
    second[:HALF] = row_pass[:HALF]
    second[SIDE:] = row_pass[HALF:SIDE]
    rows = np.stack([row_pass, first, second])
    tile_cols = np.block([[cosine, sine], [-sine, cosine]])
    proj_cols = np.block(
        [[cosine[:, :SIDE], sine[:, :SIDE]], [-sine[:, :SIDE], cosine[:, :SIDE]]]
    )
    back_cols = np.stack(
        [
            np.block(
                [
                    [cosine[part : part + HALF], -sine[part : part + HALF]],
                    [sine[part : part + HALF], cosine[part : part + HALF]],
                ]
            )
            for part in (0, HALF)
        ]
    )
    back_rows = np.concatenate([2.0 * cosine[:HALF], -2.0 * sine[:HALF]], axis=0)
    back_rows[0] = 1.0
    back_rows[HALF] = alternate
    back_rows /= EDGE
    cast = lambda table: table.astype(np.float32).astype(ml_dtypes.bfloat16)
    alt_rows = np.broadcast_to(alternate, (16, EDGE))
    flip_rows = np.eye(HALF)[::-1]
    return tuple(cast(t) for t in (rows, tile_cols, proj_cols, back_cols, back_rows, alt_rows, flip_rows))


def total_of(field):
    lines = jnp.sum(field, axis=0, keepdims=True)
    return jnp.sum(lines, axis=1, keepdims=True)


def dot(a, b):
    return jnp.dot(a, b, preferred_element_type=F32)


def kernel(
    pool_in, tile_list, counts, raw_in, rows_in, tile_cols_in, proj_cols_in, back_cols_in,
    back_rows_in, alt_in, flip_in,
    own_out, taken_out,
    pool, raw, rows, tile_cols, proj_cols, back, back_rows, alt_rows, flip_rows,
    mine, buf, chosen, landed, spec, circ, stats, held_proj, held_edge, parts,
    load_sem, send_sem, recv_sem, half_recv, tile_send, tile_recv, part_send, part_recv,
):
    me = lax.axis_index("blk")
    bank = lax.axis_index("bank")
    chip = me // 2
    core = me % 2
    odd = chip % 2
    first_plane = (chip // 2) % 8 == 0
    other = 1 - bank

    def device(ahead, which, side):
        return (((chip + ahead + CHIPS) % CHIPS) * 2 + which, side)

    sibling = device(0, 1 - core, bank)
    sources = (
        raw_in, pool_in, rows_in, alt_in, flip_in, tile_cols_in, proj_cols_in,
        back_cols_in.at[bank], back_rows_in,
    )
    targets = (raw, pool, rows, alt_rows, flip_rows, tile_cols, proj_cols, back, back_rows)
    loads = [
        pltpu.make_async_copy(source, target, load_sem.at[n])
        for n, (source, target) in enumerate(zip(sources, targets))
    ]
    loads[0].start()

    barrier = pltpu.get_barrier_semaphore()

    def greet(target):
        pl.semaphore_signal(barrier, inc=1, device_id=target, device_id_type=MESH)

    greet(sibling)
    greet(device(0, 0, other))
    greet(device(0, 1, other))
    greet(device(-2, 1, bank))
    greet(device(-2, 1, other))

    @pl.when(odd == 0)
    def _():
        greet(device(1, core, bank))
        greet(device(1, core, other))

    @pl.when(odd == 1)
    def _():
        greet(device(-2, 0, bank))
        for side in (bank, other):
            for which in (0, 1):
                greet(device(-1, which, side))

    loads[0].wait()
    for load in loads[1:]:
        load.start()
    packs = []
    for r in range(2):
        image = raw[r].astype(F32)
        centred = image - total_of(image) * (1.0 / (SIDE * SIDE))
        power = total_of(centred * centred) * (1.0 / (SIDE * SIDE))
        unit = centred * (1.0 / (SIDE * jnp.sqrt(power + 1e-5)))
        right = jnp.concatenate([unit[:96, HALF:], unit[96:, HALF:]], axis=1)
        packs.append(jnp.concatenate([unit[:, :HALF], right], axis=0))
    for r in range(2):
        mine[r] = packs[r].astype(BF16)
    buf[2 * core] = jnp.where(core == 0, packs[0], packs[1]).astype(BF16)

    @pl.when(core == 0)
    def _():
        pl.semaphore_wait(barrier, 7)

    @pl.when((odd == 1) & (core == 1))
    def _():
        pl.semaphore_wait(barrier, 9)

    @pl.when((odd == 0) & (core == 1))
    def _():
        pl.semaphore_wait(barrier, 11)

    variants = [(which, parity) for which in (0, 1) for parity in (0, 1)]
    sent = {variant: [] for variant in variants}

    def copy_of(source, target, sent_sem, got_sem, to):
        return pltpu.make_async_remote_copy(
            src_ref=source,
            dst_ref=target,
            send_sem=sent_sem,
            recv_sem=got_sem,
            device_id=to,
            device_id_type=MESH,
        )

    def send(variant, source, target, to):
        index = len(sent[variant])
        sent[variant].append(UNIT[0])
        copy_of(source, buf.at[target], send_sem.at[index], recv_sem.at[target], to).start()

    def send_piece(variant, source, piece, target, got_sem, to):
        index = len(sent[variant])
        sent[variant].append(PIECE)
        rows_of = pl.ds(piece * PIECE, PIECE)
        copy_of(
            source.at[rows_of], buf.at[target, rows_of], send_sem.at[index], got_sem, to
        ).start()

    def arrive(target):
        copy_of(buf.at[target], buf.at[target], send_sem.at[0], recv_sem.at[target], sibling).wait_recv()

    def each_variant(phase, when=True):
        for variant in variants:
            here = (core == variant[0]) & (odd == variant[1]) & when
            pl.when(here)(functools.partial(phase, variant))

    sides = ((0, bank), (1, other))

    def first(variant):
        core, odd = variant
        if odd:
            target = slot(4, 0) if core == 1 else STAGE
            for piece in range(2):
                for r in range(2):
                    got = half_recv.at[2 * (1 - core) + piece]
                    send_piece(variant, mine.at[r], piece, target, got, device(2, r, bank))
        elif core == 1:
            for r in range(2):
                send(variant, mine.at[r], slot(4, 0), device(2, r, bank))
        if core == 1:
            for r in range(2):
                send(variant, mine.at[r], slot(4, 1), device(2, r, other))
        send(variant, mine.at[1 - core], slot(core, 0), device(0, 1 - core, bank))
        for r in range(2):
            send(variant, mine.at[r], slot(core, 1), device(0, r, other))
        if not odd:
            for r in range(2):
                for at, side in sides:
                    send(variant, mine.at[r], slot(2 + core, at), device(1, r, side))

    def pass_near(variant):
        core, odd = variant
        if odd:
            for piece in range(2):
                for n, (block, at) in enumerate(((3, slot(4, 0)), (2, STAGE))):
                    rows_of = pl.ds(piece * PIECE, PIECE)
                    place = buf.at[at, rows_of]
                    got = half_recv.at[2 * n + piece]
                    copy_of(place, place, send_sem.at[0], got, sibling).wait_recv()
                    for to, side in sides:
                        target = slot(block, to)
                        send_piece(
                            variant, buf.at[at], piece, target, recv_sem.at[target],
                            device(-1, core, side),
                        )

    def finish(variant):
        for index, size in enumerate(sent[variant]):
            piece = mine.at[0, pl.ds(0, size)]
            copy_of(piece, piece, send_sem.at[index], recv_sem.at[0], sibling).wait_send()

    each_variant(first)
    loads[1].wait()
    for s in range(2):
        chosen[s] = pool[tile_list[s]]
    tile_copies = [
        pltpu.make_async_remote_copy(
            src_ref=chosen.at[s],
            dst_ref=landed.at[s],
            send_sem=tile_send.at[s],
            recv_sem=tile_recv.at[s],
            device_id=sibling,
            device_id_type=MESH,
        )
        for s in range(2)
    ]
    for copy in tile_copies:
        copy.start()

    lane = lax.broadcasted_iota(jnp.int32, (1, EDGE), 1)
    is_edge = (lane % HALF) == 0
    is_guest = counts[2 * chip] == 2
    is_first = core == 0

    stats[:, 0] = jnp.full((2, HALF, EDGE), -1e30, F32)
    stats[:, 1:] = jnp.zeros((2, 2, HALF, EDGE), F32)

    for load in loads[2:6]:
        load.wait()
    for copy in tile_copies:
        copy.wait_recv()
    here = [chosen[s].astype(F32) for s in range(2)]
    there = [landed[s].astype(F32) for s in range(2)]
    images = (
        jnp.where(is_first, here[0], there[0]),
        jnp.where(
            is_guest,
            jnp.where(is_first, here[1], there[1]),
            jnp.where(is_first, there[0], here[0]),
        ),
    )
    res, ims = [], []
    for s in range(2):
        image = images[s]
        centred = image - total_of(image) * (1.0 / (EDGE * EDGE))
        power = total_of(centred * centred) * (1.0 / (EDGE * EDGE))
        unit = (centred * (1.0 / jnp.sqrt(power + 1e-5))).astype(BF16)
        passed = dot(unit, rows[0])
        res.append(passed[:, :HALF])
        ims.append(passed[:, HALF:])
        column = lax.dot_general(
            alt_rows[...], unit, (((1,), (1,)), ((), ())), preferred_element_type=F32
        )[:8]
        swapped = jnp.concatenate([column[:, HALF:], column[:, :HALF]], axis=1)
        column = jnp.where(bank == 1, swapped, column)
        spread = jnp.broadcast_to(column[:1], (HALF, EDGE))
        spread = pltpu.roll(spread, HALF + 1, 1, stride=1, stride_axis=0)
        circ[s] = dot(flip_rows[...], spread[:, :SIDE].astype(BF16)).astype(BF16)
    tile_re = jnp.concatenate(res, axis=1).astype(BF16)
    tile_im = jnp.where(is_edge, 0.0, jnp.concatenate(ims, axis=1)).astype(BF16)
    products = dot(tile_cols[...], jnp.concatenate([tile_re, tile_im], axis=0)) * (1.0 / EDGE)
    for s in range(2):
        part = products[:, s * HALF : (s + 1) * HALF].astype(BF16)
        spec[s] = jnp.concatenate([part, part], axis=1)

    for load in loads[6:]:
        load.wait()
    before = {variant: list(sizes) for variant, sizes in sent.items()}
    each_variant(pass_near, jnp.logical_not(first_plane))
    after = dict(sent)
    sent.update(before)

    def spectra(blocks):
        units = [buf[slot(block, at)] for block in blocks for at in range(2)]
        tops = [jnp.concatenate([unit[:96], unit[SIDE:]], axis=1) for unit in units]
        bottoms = [jnp.concatenate([unit[96:SIDE], unit[SIDE:]], axis=1) for unit in units]
        top = dot(jnp.concatenate(tops, axis=0), rows[1])
        bottom = dot(jnp.concatenate(bottoms, axis=0), rows[2])
        out = []
        for n in range(len(blocks)):
            parts_re, parts_im = [], []
            for at in range(2):
                lines = slice((2 * n + at) * 96, (2 * n + at + 1) * 96)
                passed = jnp.concatenate([top[lines], bottom[lines]], axis=0)
                parts_re.append(passed[:, :HALF])
                parts_im.append(passed[:, HALF:])
            row_re = jnp.concatenate(parts_re, axis=1).astype(BF16)
            row_im = jnp.concatenate(parts_im, axis=1)
            edge = jnp.where(is_edge, row_im, 0.0).astype(BF16)
            row_im = jnp.where(is_edge, 0.0, row_im).astype(BF16)
            out.append((jnp.concatenate([row_re, row_im], axis=0), edge))
        return [(dot(proj_cols[...], row).astype(BF16), edge) for row, edge in out]

    def cross_stage(s, proj):
        proj_re, proj_im = proj[:EDGE].astype(F32), proj[EDGE:].astype(F32)
        tile_re, tile_im = spec[s, :EDGE].astype(F32), spec[s, EDGE:].astype(F32)
        cross_re = (tile_re * proj_re + tile_im * proj_im).astype(BF16)
        cross_im = (tile_im * proj_re - tile_re * proj_im).astype(BF16)
        return jnp.concatenate([cross_re, cross_im], axis=0)

    def correlate(pairs):
        crosses = [cross_stage(s, proj) for s, (proj, _) in pairs]
        inners = [dot(back[...], cross) for cross in crosses]
        extras = [dot(circ[s], edge) for s, (_, edge) in pairs]
        corrs = []
        for inner, extra in zip(inners, extras):
            inner_re = inner[:HALF].astype(BF16)
            inner_im = (inner[HALF:] + extra).astype(BF16)
            stacked = [
                jnp.concatenate([inner_re[:, lanes], inner_im[:, lanes]], axis=1)
                for lanes in (slice(0, HALF), slice(HALF, EDGE))
            ]
            corrs.append(dot(jnp.concatenate(stacked, axis=0), back_rows[...]))
        for (s, _), corr in zip(pairs, corrs):
            one, two = corr[:HALF], corr[HALF:]
            stats[s, 0] = jnp.maximum(stats[s, 0], jnp.maximum(one, two))
            stats[s, 1] = stats[s, 1] + (one + two)
            stats[s, 2] = stats[s, 2] + (one * one + two * two)

    arrive(slot(1 - core, 0))
    arrive(slot(0, 1))
    arrive(slot(1, 1))
    now, spare = spectra((0, 1))
    correlate([(0, now), (1, now)])

    def chip_before():
        for block in (3, 2):
            for at in range(2):
                arrive(slot(block, at))
        one, two = spectra((3, 2))
        correlate([(0, one), (0, two), (1, one), (1, two)])

    def two_before():
        @pl.when(odd == 0)
        def _():
            arrive(slot(4, 0))

        arrive(slot(4, 1))
        (far,) = spectra((4,))
        guest = [jnp.where(is_guest, f.astype(F32), c.astype(F32)).astype(BF16) for f, c in zip(far, held())]
        correlate([(0, far), (1, guest)])

    held_proj[...], held_edge[...] = spare

    def held():
        return held_proj[...], held_edge[...]

    each_variant(pass_near, first_plane)
    sent.update(after)

    def last_steps(step, carry):
        pl.when((step == 0) == (odd == 1))(chip_before)
        pl.when((step == 0) == (odd == 0))(two_before)
        return carry

    lax.fori_loop(0, 2, last_steps, 0)

    theirs = [
        copy_of(parts.at[s], taken_out.at[s], part_send.at[s], part_recv.at[s], sibling)
        for s in range(2)
    ]
    ours = [pltpu.make_async_copy(parts.at[s], own_out.at[s], load_sem.at[s]) for s in range(2)]
    parts[1] = stats[1].astype(BF16)
    theirs[1].start()
    parts[0] = stats[0].astype(BF16)

    @pl.when(core == 1)
    def _():
        theirs[0].start()

    @pl.when(core == 0)
    def _():
        ours[0].start()

    ours[1].start()
    each_variant(finish)
    for copy in tile_copies:
        copy.wait_send()
    theirs[1].wait()
    ours[1].wait()

    @pl.when(core == 1)
    def _():
        theirs[0].wait_send()

    @pl.when(core == 0)
    def _():
        theirs[0].wait_recv()
        ours[0].wait()


def merge_kernel(counts, own, taken, peak_out, score_out):
    me = lax.axis_index("blk")
    is_first = me % 2 == 0
    live = counts[me]
    peaks, scores = [], []
    for s in range(2):
        mine, theirs = own[s].astype(F32), taken[s].astype(F32)
        peak = jnp.maximum(mine[0], theirs[0])
        mean = (mine[1] + theirs[1]) * (1.0 / 16)
        square = (mine[2] + theirs[2]) * (1.0 / 16)
        variance = jnp.maximum(square - mean * mean, 0.3)
        peaks.append(peak)
        scores.append((peak - mean) / jnp.sqrt(variance))
    for out, maps in ((peak_out, peaks), (score_out, scores)):
        out[0] = jnp.where(live > 0, jnp.where(is_first, maps[0], maps[1]), 0.0)
        out[1] = jnp.where(live > 1, maps[1], 0.0)


def body(tile_pool, tile_list, counts, projections):
    tables = [jnp.asarray(t) for t in make_tables()]
    any_spec = pl.BlockSpec(memory_space=pl.ANY)
    vmem = pl.BlockSpec(memory_space=pltpu.VMEM)
    smem = pl.BlockSpec(memory_space=pltpu.SMEM)
    own, taken = pl.pallas_call(
        kernel,
        out_shape=(
            jax.ShapeDtypeStruct((2, 3, HALF, EDGE), BF16),
            jax.ShapeDtypeStruct((2, 3, HALF, EDGE), BF16),
        ),
        in_specs=[any_spec, smem, smem] + [any_spec] * 8,
        out_specs=(any_spec, any_spec),
        scratch_shapes=[
            pltpu.VMEM((4, EDGE, EDGE), BF16),
            pltpu.VMEM((2, SIDE, SIDE), BF16),
            pltpu.VMEM((3, EDGE, EDGE), BF16),
            pltpu.VMEM((2 * EDGE, 2 * EDGE), BF16),
            pltpu.VMEM((2 * EDGE, 2 * SIDE), BF16),
            pltpu.VMEM((EDGE, 2 * EDGE), BF16),
            pltpu.VMEM((EDGE, EDGE), BF16),
            pltpu.VMEM((16, EDGE), BF16),
            pltpu.VMEM((HALF, HALF), BF16),
            pltpu.VMEM((2,) + UNIT, BF16),
            pltpu.VMEM((STAGE + 1,) + UNIT, BF16),
            pltpu.VMEM((2, EDGE, EDGE), BF16),
            pltpu.VMEM((2, EDGE, EDGE), BF16),
            pltpu.VMEM((2, 2 * EDGE, EDGE), BF16),
            pltpu.VMEM((2, HALF, SIDE), BF16),
            pltpu.VMEM((2, 3, HALF, EDGE), F32),
            pltpu.VMEM((2 * EDGE, EDGE), BF16),
            pltpu.VMEM((SIDE, EDGE), BF16),
            pltpu.VMEM((2, 3, HALF, EDGE), BF16),
            pltpu.SemaphoreType.DMA((9,)),
            pltpu.SemaphoreType.DMA((20,)),
            pltpu.SemaphoreType.DMA((STAGE + 1,)),
            pltpu.SemaphoreType.DMA((4,)),
            pltpu.SemaphoreType.DMA((2,)),
            pltpu.SemaphoreType.DMA((2,)),
            pltpu.SemaphoreType.DMA((2,)),
            pltpu.SemaphoreType.DMA((2,)),
        ],
        compiler_params=pltpu.CompilerParams(
            collective_id=0, has_side_effects=True, vmem_limit_bytes=56 << 20
        ),
    )(tile_pool, tile_list, counts, projections, *tables)
    out = jax.ShapeDtypeStruct((2, HALF, EDGE), F32)
    part = pl.BlockSpec((2, 3, HALF // 2, EDGE), lambda i: (0, 0, i, 0))
    out_part = pl.BlockSpec((2, HALF // 2, EDGE), lambda i: (0, i, 0))
    return pl.pallas_call(
        merge_kernel,
        grid=(2,),
        out_shape=(out, out),
        in_specs=[smem, part, part],
        out_specs=(out_part, out_part),
    )(counts, own, taken)


def solution(mesh):
    in_specs = (P("blk", None, None), P("blk"), P(), P(("blk", "bank"), None, None))
    out_specs = (P("blk", "bank", None), P("blk", "bank", None))
    return jax.shard_map(body, mesh=mesh, in_specs=in_specs, out_specs=out_specs, check_vma=False)
```

```python
import functools

import jax
import jax.numpy as jnp
import ml_dtypes
import numpy as np
from jax import lax
from jax.experimental import pallas as pl
from jax.experimental.pallas import tpu as pltpu
from jax.sharding import PartitionSpec as P

EDGE = 256
SIDE = 192
HALF = 128
CHIPS = 64
UNIT = (288, 128)
PIECES = 3
PIECE = UNIT[0] // PIECES
BF16 = jnp.bfloat16
F32 = jnp.float32
MESH = pl.DeviceIdType.MESH
STAGE = 10


def slot(block, at):
    return block * 2 + at


def make_tables():
    index = np.arange(EDGE)
    angle = (index[:, None] * index[None, :] % EDGE) * (2.0 * np.pi / EDGE)
    cosine = np.cos(angle)
    sine = np.sin(angle)
    alternate = 1.0 - 2.0 * (index % 2)
    row_pass = np.concatenate([cosine[:, :HALF], -sine[:, :HALF]], axis=1)
    row_pass[:, HALF] = alternate
    first = np.zeros((EDGE, EDGE))
    first[:SIDE] = row_pass[:SIDE]
    second = np.zeros((EDGE, EDGE))
    second[:HALF] = row_pass[:HALF]
    second[SIDE:] = row_pass[HALF:SIDE]
    rows = np.stack([row_pass, first, second])
    tile_cols = np.block([[cosine, sine], [-sine, cosine]])
    proj_cols = np.block(
        [[cosine[:, :SIDE], sine[:, :SIDE]], [-sine[:, :SIDE], cosine[:, :SIDE]]]
    )
    back_cols = np.stack(
        [
            np.block(
                [
                    [cosine[part : part + HALF], -sine[part : part + HALF]],
                    [sine[part : part + HALF], cosine[part : part + HALF]],
                ]
            )
            for part in (0, HALF)
        ]
    )
    back_rows = np.concatenate([2.0 * cosine[:HALF], -2.0 * sine[:HALF]], axis=0)
    back_rows[0] = 1.0
    back_rows[HALF] = alternate
    back_rows /= EDGE
    cast = lambda table: table.astype(np.float32).astype(ml_dtypes.bfloat16)
    alt_rows = np.broadcast_to(alternate, (16, EDGE))
    flip_rows = np.eye(HALF)[::-1]
    return tuple(cast(t) for t in (rows, tile_cols, proj_cols, back_cols, back_rows, alt_rows, flip_rows))


def total_of(field):
    lines = jnp.sum(field, axis=0, keepdims=True)
    return jnp.sum(lines, axis=1, keepdims=True)


def dot(a, b):
    return jnp.dot(a, b, preferred_element_type=F32)


def kernel(
    pool_in, tile_list, counts, raw_in, rows_in, tile_cols_in, proj_cols_in, back_cols_in,
    back_rows_in, alt_in, flip_in,
    own_out, taken_out,
    pool, raw, rows, tile_cols, proj_cols, back, back_rows, alt_rows, flip_rows,
    mine, buf, chosen, landed, spec, circ, stats, held_proj, held_edge, parts,
    load_sem, send_sem, recv_sem, half_recv, tile_send, tile_recv, part_send, part_recv,
):
    me = lax.axis_index("blk")
    bank = lax.axis_index("bank")
    chip = me // 2
    core = me % 2
    odd = chip % 2
    first_plane = (chip // 2) % 8 == 0
    other = 1 - bank

    def device(ahead, which, side):
        return (((chip + ahead + CHIPS) % CHIPS) * 2 + which, side)

    sibling = device(0, 1 - core, bank)
    sources = (
        raw_in, pool_in, rows_in, alt_in, flip_in, tile_cols_in, proj_cols_in,
        back_cols_in.at[bank], back_rows_in,
    )
    targets = (raw, pool, rows, alt_rows, flip_rows, tile_cols, proj_cols, back, back_rows)
    loads = [
        pltpu.make_async_copy(source, target, load_sem.at[n])
        for n, (source, target) in enumerate(zip(sources, targets))
    ]
    loads[0].start()

    barrier = pltpu.get_barrier_semaphore()

    def greet(target):
        pl.semaphore_signal(barrier, inc=1, device_id=target, device_id_type=MESH)

    @pl.when(odd == 0)
    def _():
        greet(device(1, core, bank))
        greet(device(1, core, other))

    @pl.when(odd == 1)
    def _():
        for which in (0, 1):
            for side in (bank, other):
                greet(device(-1, which, side))

    greet(device(0, 0, other))
    greet(device(0, 1, other))
    greet(sibling)
    greet(device(-2, 1, bank))
    greet(device(-2, 1, other))

    @pl.when(odd == 1)
    def _():
        greet(device(-2, 0, bank))

    loads[0].wait()
    for load in loads[1:]:
        load.start()
    packs = []
    for r in range(2):
        image = raw[r].astype(F32)
        centred = image - total_of(image) * (1.0 / (SIDE * SIDE))
        power = total_of(centred * centred) * (1.0 / (SIDE * SIDE))
        unit = centred * (1.0 / (SIDE * jnp.sqrt(power + 1e-5)))
        right = jnp.concatenate([unit[:96, HALF:], unit[96:, HALF:]], axis=1)
        packs.append(jnp.concatenate([unit[:, :HALF], right], axis=0))
    for r in range(2):
        mine[r] = packs[r].astype(BF16)
    buf[2 * core] = jnp.where(core == 0, packs[0], packs[1]).astype(BF16)

    @pl.when(core == 0)
    def _():
        pl.semaphore_wait(barrier, 7)

    @pl.when((odd == 1) & (core == 1))
    def _():
        pl.semaphore_wait(barrier, 9)

    @pl.when((odd == 0) & (core == 1))
    def _():
        pl.semaphore_wait(barrier, 11)

    variants = [(which, parity) for which in (0, 1) for parity in (0, 1)]
    sent = {variant: [] for variant in variants}

    def copy_of(source, target, sent_sem, got_sem, to):
        return pltpu.make_async_remote_copy(
            src_ref=source,
            dst_ref=target,
            send_sem=sent_sem,
            recv_sem=got_sem,
            device_id=to,
            device_id_type=MESH,
        )

    def send(variant, source, target, to):
        index = len(sent[variant])
        sent[variant].append(UNIT[0])
        copy_of(source, buf.at[target], send_sem.at[index], recv_sem.at[target], to).start()

    def send_piece(variant, source, piece, target, got_sem, to):
        index = len(sent[variant])
        sent[variant].append(PIECE)
        rows_of = pl.ds(piece * PIECE, PIECE)
        copy_of(
            source.at[rows_of], buf.at[target, rows_of], send_sem.at[index], got_sem, to
        ).start()

    def arrive(target):
        copy_of(buf.at[target], buf.at[target], send_sem.at[0], recv_sem.at[target], sibling).wait_recv()

    def each_variant(phase, when=True):
        for variant in variants:
            here = (core == variant[0]) & (odd == variant[1]) & when
            pl.when(here)(functools.partial(phase, variant))

    sides = ((0, bank), (1, other))

    def first(variant):
        core, odd = variant
        if odd:
            target = slot(4, 0) if core == 1 else STAGE
            for piece in range(PIECES):
                for r in range(2):
                    got = half_recv.at[PIECES * (1 - core) + piece]
                    send_piece(variant, mine.at[r], piece, target, got, device(2, r, bank))
        elif core == 1:
            for r in range(2):
                send(variant, mine.at[r], slot(4, 0), device(2, r, bank))
        if core == 1:
            for r in range(2):
                send(variant, mine.at[r], slot(4, 1), device(2, r, other))
        send(variant, mine.at[1 - core], slot(core, 0), device(0, 1 - core, bank))
        for r in range(2):
            send(variant, mine.at[r], slot(core, 1), device(0, r, other))
        if not odd:
            for r in range(2):
                for at, side in sides:
                    send(variant, mine.at[r], slot(2 + core, at), device(1, r, side))

    def pass_near(variant):
        core, odd = variant
        if odd:
            for piece in range(PIECES):
                for n, (block, at) in enumerate(((3, slot(4, 0)), (2, STAGE))):
                    rows_of = pl.ds(piece * PIECE, PIECE)
                    place = buf.at[at, rows_of]
                    got = half_recv.at[PIECES * n + piece]
                    copy_of(place, place, send_sem.at[0], got, sibling).wait_recv()
                    for to, side in sides:
                        target = slot(block, to)
                        send_piece(
                            variant, buf.at[at], piece, target, recv_sem.at[target],
                            device(-1, core, side),
                        )

    def finish(variant):
        for index, size in enumerate(sent[variant]):
            piece = mine.at[0, pl.ds(0, size)]
            copy_of(piece, piece, send_sem.at[index], recv_sem.at[0], sibling).wait_send()

    each_variant(first)
    loads[1].wait()
    for s in range(2):
        chosen[s] = pool[tile_list[s]]
    tile_copies = [
        pltpu.make_async_remote_copy(
            src_ref=chosen.at[s],
            dst_ref=landed.at[s],
            send_sem=tile_send.at[s],
            recv_sem=tile_recv.at[s],
            device_id=sibling,
            device_id_type=MESH,
        )
        for s in range(2)
    ]
    for copy in tile_copies:
        copy.start()

    lane = lax.broadcasted_iota(jnp.int32, (1, EDGE), 1)
    is_edge = (lane % HALF) == 0
    is_guest = counts[2 * chip] == 2
    is_first = core == 0

    stats[:, 0] = jnp.full((2, HALF, EDGE), -1e30, F32)
    stats[:, 1:] = jnp.zeros((2, 2, HALF, EDGE), F32)

    for load in loads[2:6]:
        load.wait()
    for copy in tile_copies:
        copy.wait_recv()
    here = [chosen[s].astype(F32) for s in range(2)]
    there = [landed[s].astype(F32) for s in range(2)]
    images = (
        jnp.where(is_first, here[0], there[0]),
        jnp.where(
            is_guest,
            jnp.where(is_first, here[1], there[1]),
            jnp.where(is_first, there[0], here[0]),
        ),
    )
    res, ims = [], []
    for s in range(2):
        image = images[s]
        centred = image - total_of(image) * (1.0 / (EDGE * EDGE))
        power = total_of(centred * centred) * (1.0 / (EDGE * EDGE))
        unit = (centred * (1.0 / jnp.sqrt(power + 1e-5))).astype(BF16)
        passed = dot(unit, rows[0])
        res.append(passed[:, :HALF])
        ims.append(passed[:, HALF:])
        column = lax.dot_general(
            alt_rows[...], unit, (((1,), (1,)), ((), ())), preferred_element_type=F32
        )[:8]
        swapped = jnp.concatenate([column[:, HALF:], column[:, :HALF]], axis=1)
        column = jnp.where(bank == 1, swapped, column)
        spread = jnp.broadcast_to(column[:1], (HALF, EDGE))
        spread = pltpu.roll(spread, HALF + 1, 1, stride=1, stride_axis=0)
        circ[s] = dot(flip_rows[...], spread[:, :SIDE].astype(BF16)).astype(BF16)
    tile_re = jnp.concatenate(res, axis=1).astype(BF16)
    tile_im = jnp.where(is_edge, 0.0, jnp.concatenate(ims, axis=1)).astype(BF16)
    products = dot(tile_cols[...], jnp.concatenate([tile_re, tile_im], axis=0)) * (1.0 / EDGE)
    for s in range(2):
        part = products[:, s * HALF : (s + 1) * HALF].astype(BF16)
        spec[s] = jnp.concatenate([part, part], axis=1)

    for load in loads[6:]:
        load.wait()
    before = {variant: list(sizes) for variant, sizes in sent.items()}
    each_variant(pass_near, jnp.logical_not(first_plane))
    after = dict(sent)
    sent.update(before)

    def spectra(blocks):
        units = [buf[slot(block, at)] for block in blocks for at in range(2)]
        tops = [jnp.concatenate([unit[:96], unit[SIDE:]], axis=1) for unit in units]
        bottoms = [jnp.concatenate([unit[96:SIDE], unit[SIDE:]], axis=1) for unit in units]
        top = dot(jnp.concatenate(tops, axis=0), rows[1])
        bottom = dot(jnp.concatenate(bottoms, axis=0), rows[2])
        out = []
        for n in range(len(blocks)):
            parts_re, parts_im = [], []
            for at in range(2):
                lines = slice((2 * n + at) * 96, (2 * n + at + 1) * 96)
                passed = jnp.concatenate([top[lines], bottom[lines]], axis=0)
                parts_re.append(passed[:, :HALF])
                parts_im.append(passed[:, HALF:])
            row_re = jnp.concatenate(parts_re, axis=1).astype(BF16)
            row_im = jnp.concatenate(parts_im, axis=1)
            edge = jnp.where(is_edge, row_im, 0.0).astype(BF16)
            row_im = jnp.where(is_edge, 0.0, row_im).astype(BF16)
            out.append((jnp.concatenate([row_re, row_im], axis=0), edge))
        return [(dot(proj_cols[...], row).astype(BF16), edge) for row, edge in out]

    def cross_stage(s, proj):
        proj_re, proj_im = proj[:EDGE].astype(F32), proj[EDGE:].astype(F32)
        tile_re, tile_im = spec[s, :EDGE].astype(F32), spec[s, EDGE:].astype(F32)
        cross_re = (tile_re * proj_re + tile_im * proj_im).astype(BF16)
        cross_im = (tile_im * proj_re - tile_re * proj_im).astype(BF16)
        return jnp.concatenate([cross_re, cross_im], axis=0)

    def correlate(pairs):
        crosses = [cross_stage(s, proj) for s, (proj, _) in pairs]
        inners = [dot(back[...], cross) for cross in crosses]
        extras = [dot(circ[s], edge) for s, (_, edge) in pairs]
        corrs = []
        for inner, extra in zip(inners, extras):
            inner_re = inner[:HALF].astype(BF16)
            inner_im = (inner[HALF:] + extra).astype(BF16)
            stacked = [
                jnp.concatenate([inner_re[:, lanes], inner_im[:, lanes]], axis=1)
                for lanes in (slice(0, HALF), slice(HALF, EDGE))
            ]
            corrs.append(dot(jnp.concatenate(stacked, axis=0), back_rows[...]))
        for (s, _), corr in zip(pairs, corrs):
            one, two = corr[:HALF], corr[HALF:]
            stats[s, 0] = jnp.maximum(stats[s, 0], jnp.maximum(one, two))
            stats[s, 1] = stats[s, 1] + (one + two)
            stats[s, 2] = stats[s, 2] + (one * one + two * two)

    arrive(slot(1 - core, 0))
    arrive(slot(0, 1))
    arrive(slot(1, 1))
    now, spare = spectra((0, 1))
    correlate([(0, now), (1, now)])

    def chip_before():
        for block in (3, 2):
            for at in range(2):
                arrive(slot(block, at))
        one, two = spectra((3, 2))
        correlate([(1, one), (1, two), (0, one), (0, two)])

    def two_before():
        @pl.when(odd == 0)
        def _():
            arrive(slot(4, 0))

        arrive(slot(4, 1))
        (far,) = spectra((4,))
        guest = [jnp.where(is_guest, f.astype(F32), c.astype(F32)).astype(BF16) for f, c in zip(far, held())]
        correlate([(0, far), (1, guest)])

    held_proj[...], held_edge[...] = spare

    def held():
        return held_proj[...], held_edge[...]

    each_variant(pass_near, first_plane)
    sent.update(after)

    def last_steps(step, carry):
        pl.when((step == 0) == (odd == 1))(chip_before)
        pl.when((step == 0) == (odd == 0))(two_before)
        return carry

    lax.fori_loop(0, 2, last_steps, 0)

    theirs = [
        copy_of(parts.at[s], taken_out.at[s], part_send.at[s], part_recv.at[s], sibling)
        for s in range(2)
    ]
    ours = [pltpu.make_async_copy(parts.at[s], own_out.at[s], load_sem.at[s]) for s in range(2)]
    parts[1] = stats[1].astype(BF16)
    theirs[1].start()
    parts[0] = stats[0].astype(BF16)

    @pl.when(core == 1)
    def _():
        theirs[0].start()

    @pl.when(core == 0)
    def _():
        ours[0].start()

    ours[1].start()
    each_variant(finish)
    for copy in tile_copies:
        copy.wait_send()
    theirs[1].wait()
    ours[1].wait()

    @pl.when(core == 1)
    def _():
        theirs[0].wait_send()

    @pl.when(core == 0)
    def _():
        theirs[0].wait_recv()
        ours[0].wait()


def merge_kernel(counts, own, taken, peak_out, score_out):
    me = lax.axis_index("blk")
    is_first = me % 2 == 0
    live = counts[me]
    peaks, scores = [], []
    for s in range(2):
        mine, theirs = own[s].astype(F32), taken[s].astype(F32)
        peak = jnp.maximum(mine[0], theirs[0])
        mean = (mine[1] + theirs[1]) * (1.0 / 16)
        square = (mine[2] + theirs[2]) * (1.0 / 16)
        variance = jnp.maximum(square - mean * mean, 0.3)
        peaks.append(peak)
        scores.append((peak - mean) / jnp.sqrt(variance))
    for out, maps in ((peak_out, peaks), (score_out, scores)):
        out[0] = jnp.where(live > 0, jnp.where(is_first, maps[0], maps[1]), 0.0)
        out[1] = jnp.where(live > 1, maps[1], 0.0)


def body(tile_pool, tile_list, counts, projections):
    tables = [jnp.asarray(t) for t in make_tables()]
    any_spec = pl.BlockSpec(memory_space=pl.ANY)
    vmem = pl.BlockSpec(memory_space=pltpu.VMEM)
    smem = pl.BlockSpec(memory_space=pltpu.SMEM)
    own, taken = pl.pallas_call(
        kernel,
        out_shape=(
            jax.ShapeDtypeStruct((2, 3, HALF, EDGE), BF16),
            jax.ShapeDtypeStruct((2, 3, HALF, EDGE), BF16),
        ),
        in_specs=[any_spec, smem, smem] + [any_spec] * 8,
        out_specs=(any_spec, any_spec),
        scratch_shapes=[
            pltpu.VMEM((4, EDGE, EDGE), BF16),
            pltpu.VMEM((2, SIDE, SIDE), BF16),
            pltpu.VMEM((3, EDGE, EDGE), BF16),
            pltpu.VMEM((2 * EDGE, 2 * EDGE), BF16),
            pltpu.VMEM((2 * EDGE, 2 * SIDE), BF16),
            pltpu.VMEM((EDGE, 2 * EDGE), BF16),
            pltpu.VMEM((EDGE, EDGE), BF16),
            pltpu.VMEM((16, EDGE), BF16),
            pltpu.VMEM((HALF, HALF), BF16),
            pltpu.VMEM((2,) + UNIT, BF16),
            pltpu.VMEM((STAGE + 1,) + UNIT, BF16),
            pltpu.VMEM((2, EDGE, EDGE), BF16),
            pltpu.VMEM((2, EDGE, EDGE), BF16),
            pltpu.VMEM((2, 2 * EDGE, EDGE), BF16),
            pltpu.VMEM((2, HALF, SIDE), BF16),
            pltpu.VMEM((2, 3, HALF, EDGE), F32),
            pltpu.VMEM((2 * EDGE, EDGE), BF16),
            pltpu.VMEM((SIDE, EDGE), BF16),
            pltpu.VMEM((2, 3, HALF, EDGE), BF16),
            pltpu.SemaphoreType.DMA((9,)),
            pltpu.SemaphoreType.DMA((32,)),
            pltpu.SemaphoreType.DMA((STAGE + 1,)),
            pltpu.SemaphoreType.DMA((2 * PIECES,)),
            pltpu.SemaphoreType.DMA((2,)),
            pltpu.SemaphoreType.DMA((2,)),
            pltpu.SemaphoreType.DMA((2,)),
            pltpu.SemaphoreType.DMA((2,)),
        ],
        compiler_params=pltpu.CompilerParams(
            collective_id=0, has_side_effects=True, vmem_limit_bytes=56 << 20
        ),
    )(tile_pool, tile_list, counts, projections, *tables)
    out = jax.ShapeDtypeStruct((2, HALF, EDGE), F32)
    part = pl.BlockSpec((2, 3, HALF // 2, EDGE), lambda i: (0, 0, i, 0))
    out_part = pl.BlockSpec((2, HALF // 2, EDGE), lambda i: (0, i, 0))
    return pl.pallas_call(
        merge_kernel,
        grid=(2,),
        out_shape=(out, out),
        in_specs=[smem, part, part],
        out_specs=(out_part, out_part),
    )(counts, own, taken)


def solution(mesh):
    in_specs = (P("blk", None, None), P("blk"), P(), P(("blk", "bank"), None, None))
    out_specs = (P("blk", "bank", None), P("blk", "bank", None))
    return jax.shard_map(body, mesh=mesh, in_specs=in_specs, out_specs=out_specs, check_vma=False)
```

```python
import functools

import jax
import jax.numpy as jnp
import ml_dtypes
import numpy as np
from jax import lax
from jax.experimental import pallas as pl
from jax.experimental.pallas import tpu as pltpu
from jax.sharding import PartitionSpec as P

EDGE = 256
SIDE = 192
HALF = 128
CHIPS = 64
UNIT = (288, 128)
PIECES = 3
PIECE = UNIT[0] // PIECES
BF16 = jnp.bfloat16
F32 = jnp.float32
MESH = pl.DeviceIdType.MESH
STAGE = 10


def slot(block, at):
    return block * 2 + at


def make_tables():
    index = np.arange(EDGE)
    angle = (index[:, None] * index[None, :] % EDGE) * (2.0 * np.pi / EDGE)
    cosine = np.cos(angle)
    sine = np.sin(angle)
    alternate = 1.0 - 2.0 * (index % 2)
    row_pass = np.concatenate([cosine[:, :HALF], -sine[:, :HALF]], axis=1)
    row_pass[:, HALF] = alternate
    first = np.zeros((EDGE, EDGE))
    first[:SIDE] = row_pass[:SIDE]
    second = np.zeros((EDGE, EDGE))
    second[:HALF] = row_pass[:HALF]
    second[SIDE:] = row_pass[HALF:SIDE]
    rows = np.stack([row_pass, first, second])
    tile_cols = np.block([[cosine, sine], [-sine, cosine]])
    proj_cols = np.block(
        [[cosine[:, :SIDE], sine[:, :SIDE]], [-sine[:, :SIDE], cosine[:, :SIDE]]]
    )
    back_cols = np.stack(
        [
            np.block(
                [
                    [cosine[part : part + HALF], -sine[part : part + HALF]],
                    [sine[part : part + HALF], cosine[part : part + HALF]],
                ]
            )
            for part in (0, HALF)
        ]
    )
    back_rows = np.concatenate([2.0 * cosine[:HALF], -2.0 * sine[:HALF]], axis=0)
    back_rows[0] = 1.0
    back_rows[HALF] = alternate
    back_rows /= EDGE
    cast = lambda table: table.astype(np.float32).astype(ml_dtypes.bfloat16)
    alt_rows = np.broadcast_to(alternate, (16, EDGE))
    flip_rows = np.eye(HALF)[::-1]
    return tuple(cast(t) for t in (rows, tile_cols, proj_cols, back_cols, back_rows, alt_rows, flip_rows))


def total_of(field):
    lines = jnp.sum(field, axis=0, keepdims=True)
    return jnp.sum(lines, axis=1, keepdims=True)


def dot(a, b):
    return jnp.dot(a, b, preferred_element_type=F32)


def kernel(
    pool_in, tile_list, counts, raw_in, rows_in, tile_cols_in, proj_cols_in, back_cols_in,
    back_rows_in, alt_in, flip_in,
    own_out, taken_out,
    pool, raw, rows, tile_cols, proj_cols, back, back_rows, alt_rows, flip_rows,
    mine, buf, chosen, landed, spec, circ, stats, held_proj, held_edge, parts,
    load_sem, send_sem, recv_sem, half_recv, tile_send, tile_recv, part_send, part_recv,
):
    me = lax.axis_index("blk")
    bank = lax.axis_index("bank")
    chip = me // 2
    core = me % 2
    odd = chip % 2
    first_plane = (chip // 2) % 8 == 0
    other = 1 - bank

    def device(ahead, which, side):
        return (((chip + ahead + CHIPS) % CHIPS) * 2 + which, side)

    sibling = device(0, 1 - core, bank)
    sources = (
        raw_in, pool_in, rows_in, alt_in, flip_in, tile_cols_in, proj_cols_in,
        back_cols_in.at[bank], back_rows_in,
    )
    targets = (raw, pool, rows, alt_rows, flip_rows, tile_cols, proj_cols, back, back_rows)
    loads = [
        pltpu.make_async_copy(source, target, load_sem.at[n])
        for n, (source, target) in enumerate(zip(sources, targets))
    ]
    loads[0].start()

    barrier = pltpu.get_barrier_semaphore()

    def greet(target):
        pl.semaphore_signal(barrier, inc=1, device_id=target, device_id_type=MESH)

    @pl.when(odd == 0)
    def _():
        greet(device(1, core, bank))
        greet(device(1, core, other))

    @pl.when(odd == 1)
    def _():
        for which in (0, 1):
            for side in (bank, other):
                greet(device(-1, which, side))

    greet(device(0, 0, other))
    greet(device(0, 1, other))
    greet(sibling)
    greet(device(-2, 1, bank))
    greet(device(-2, 1, other))

    @pl.when(odd == 1)
    def _():
        greet(device(-2, 0, bank))

    loads[0].wait()
    for load in loads[1:]:
        load.start()
    packs = []
    for r in range(2):
        image = raw[r].astype(F32)
        centred = image - total_of(image) * (1.0 / (SIDE * SIDE))
        power = total_of(centred * centred) * (1.0 / (SIDE * SIDE))
        unit = centred * (1.0 / (SIDE * jnp.sqrt(power + 1e-5)))
        right = jnp.concatenate([unit[:96, HALF:], unit[96:, HALF:]], axis=1)
        packs.append(jnp.concatenate([unit[:, :HALF], right], axis=0))
    for r in range(2):
        mine[r] = packs[r].astype(BF16)
    buf[2 * core] = jnp.where(core == 0, packs[0], packs[1]).astype(BF16)

    @pl.when(core == 0)
    def _():
        pl.semaphore_wait(barrier, 7)

    @pl.when((odd == 1) & (core == 1))
    def _():
        pl.semaphore_wait(barrier, 9)

    @pl.when((odd == 0) & (core == 1))
    def _():
        pl.semaphore_wait(barrier, 11)

    variants = [(which, parity) for which in (0, 1) for parity in (0, 1)]
    sent = {variant: [] for variant in variants}

    def copy_of(source, target, sent_sem, got_sem, to):
        return pltpu.make_async_remote_copy(
            src_ref=source,
            dst_ref=target,
            send_sem=sent_sem,
            recv_sem=got_sem,
            device_id=to,
            device_id_type=MESH,
        )

    def send(variant, source, target, to):
        index = len(sent[variant])
        sent[variant].append(UNIT[0])
        copy_of(source, buf.at[target], send_sem.at[index], recv_sem.at[target], to).start()

    def send_piece(variant, source, piece, target, got_sem, to):
        index = len(sent[variant])
        sent[variant].append(PIECE)
        rows_of = pl.ds(piece * PIECE, PIECE)
        copy_of(
            source.at[rows_of], buf.at[target, rows_of], send_sem.at[index], got_sem, to
        ).start()

    def arrive(target):
        copy_of(buf.at[target], buf.at[target], send_sem.at[0], recv_sem.at[target], sibling).wait_recv()

    def each_variant(phase, when=True):
        for variant in variants:
            here = (core == variant[0]) & (odd == variant[1]) & when
            pl.when(here)(functools.partial(phase, variant))

    sides = ((0, bank), (1, other))

    def first(variant):
        core, odd = variant
        if odd:
            target = slot(4, 0) if core == 1 else STAGE
            for piece in range(PIECES):
                for r in range(2):
                    got = half_recv.at[PIECES * (1 - core) + piece]
                    send_piece(variant, mine.at[r], piece, target, got, device(2, r, bank))
        elif core == 1:
            for r in range(2):
                send(variant, mine.at[r], slot(4, 0), device(2, r, bank))
        if core == 1:
            for r in range(2):
                send(variant, mine.at[r], slot(4, 1), device(2, r, other))
        send(variant, mine.at[1 - core], slot(core, 0), device(0, 1 - core, bank))
        for r in range(2):
            send(variant, mine.at[r], slot(core, 1), device(0, r, other))
        if not odd:
            for r in range(2):
                for at, side in sides:
                    send(variant, mine.at[r], slot(2 + core, at), device(1, r, side))

    def pass_near(variant):
        core, odd = variant
        if odd:
            for piece in range(PIECES):
                for n, (block, at) in enumerate(((3, slot(4, 0)), (2, STAGE))):
                    rows_of = pl.ds(piece * PIECE, PIECE)
                    place = buf.at[at, rows_of]
                    got = half_recv.at[PIECES * n + piece]
                    copy_of(place, place, send_sem.at[0], got, sibling).wait_recv()
                    for to, side in sides:
                        target = slot(block, to)
                        send_piece(
                            variant, buf.at[at], piece, target, recv_sem.at[target],
                            device(-1, core, side),
                        )

    def finish(variant):
        for index, size in enumerate(sent[variant]):
            piece = mine.at[0, pl.ds(0, size)]
            copy_of(piece, piece, send_sem.at[index], recv_sem.at[0], sibling).wait_send()

    each_variant(first)
    loads[1].wait()
    for s in range(2):
        chosen[s] = pool[tile_list[s]]
    tile_copies = [
        pltpu.make_async_remote_copy(
            src_ref=chosen.at[s],
            dst_ref=landed.at[s],
            send_sem=tile_send.at[s],
            recv_sem=tile_recv.at[s],
            device_id=sibling,
            device_id_type=MESH,
        )
        for s in range(2)
    ]
    for copy in tile_copies:
        copy.start()

    lane = lax.broadcasted_iota(jnp.int32, (1, EDGE), 1)
    is_edge = (lane % HALF) == 0
    is_guest = counts[2 * chip] == 2
    is_first = core == 0

    stats[:, 0] = jnp.full((2, HALF, EDGE), -1e30, F32)
    stats[:, 1:] = jnp.zeros((2, 2, HALF, EDGE), F32)

    for load in loads[2:6]:
        load.wait()
    for copy in tile_copies:
        copy.wait_recv()
    here = [chosen[s].astype(F32) for s in range(2)]
    there = [landed[s].astype(F32) for s in range(2)]
    images = (
        jnp.where(is_first, here[0], there[0]),
        jnp.where(
            is_guest,
            jnp.where(is_first, here[1], there[1]),
            jnp.where(is_first, there[0], here[0]),
        ),
    )
    res, ims = [], []
    for s in range(2):
        image = images[s]
        centred = image - total_of(image) * (1.0 / (EDGE * EDGE))
        power = total_of(centred * centred) * (1.0 / (EDGE * EDGE))
        unit = (centred * (1.0 / jnp.sqrt(power + 1e-5))).astype(BF16)
        passed = dot(unit, rows[0])
        res.append(passed[:, :HALF])
        ims.append(passed[:, HALF:])
        column = lax.dot_general(
            alt_rows[...], unit, (((1,), (1,)), ((), ())), preferred_element_type=F32
        )[:8]
        swapped = jnp.concatenate([column[:, HALF:], column[:, :HALF]], axis=1)
        column = jnp.where(bank == 1, swapped, column)
        spread = jnp.broadcast_to(column[:1], (HALF, EDGE))
        spread = pltpu.roll(spread, HALF + 1, 1, stride=1, stride_axis=0)
        circ[s] = dot(flip_rows[...], spread[:, :SIDE].astype(BF16)).astype(BF16)
    tile_re = jnp.concatenate(res, axis=1).astype(BF16)
    tile_im = jnp.where(is_edge, 0.0, jnp.concatenate(ims, axis=1)).astype(BF16)
    products = dot(tile_cols[...], jnp.concatenate([tile_re, tile_im], axis=0)) * (1.0 / EDGE)
    for s in range(2):
        part = products[:, s * HALF : (s + 1) * HALF].astype(BF16)
        spec[s] = jnp.concatenate([part, part], axis=1)

    for load in loads[6:]:
        load.wait()
    before = {variant: list(sizes) for variant, sizes in sent.items()}
    each_variant(pass_near, jnp.logical_not(first_plane))
    after = dict(sent)
    sent.update(before)

    def spectra(blocks):
        units = [buf[slot(block, at)] for block in blocks for at in range(2)]
        tops = [jnp.concatenate([unit[:96], unit[SIDE:]], axis=1) for unit in units]
        bottoms = [jnp.concatenate([unit[96:SIDE], unit[SIDE:]], axis=1) for unit in units]
        top = dot(jnp.concatenate(tops, axis=0), rows[1])
        bottom = dot(jnp.concatenate(bottoms, axis=0), rows[2])
        out = []
        for n in range(len(blocks)):
            parts_re, parts_im = [], []
            for at in range(2):
                lines = slice((2 * n + at) * 96, (2 * n + at + 1) * 96)
                passed = jnp.concatenate([top[lines], bottom[lines]], axis=0)
                parts_re.append(passed[:, :HALF])
                parts_im.append(passed[:, HALF:])
            row_re = jnp.concatenate(parts_re, axis=1).astype(BF16)
            row_im = jnp.concatenate(parts_im, axis=1)
            edge = jnp.where(is_edge, row_im, 0.0).astype(BF16)
            row_im = jnp.where(is_edge, 0.0, row_im).astype(BF16)
            out.append((jnp.concatenate([row_re, row_im], axis=0), edge))
        return [(dot(proj_cols[...], row).astype(BF16), edge) for row, edge in out]

    def cross_stage(s, proj):
        proj_re, proj_im = proj[:EDGE].astype(F32), proj[EDGE:].astype(F32)
        tile_re, tile_im = spec[s, :EDGE].astype(F32), spec[s, EDGE:].astype(F32)
        cross_re = (tile_re * proj_re + tile_im * proj_im).astype(BF16)
        cross_im = (tile_im * proj_re - tile_re * proj_im).astype(BF16)
        return jnp.concatenate([cross_re, cross_im], axis=0)

    def correlate(pairs):
        crosses = [cross_stage(s, proj) for s, (proj, _) in pairs]
        inners = [dot(back[...], cross) for cross in crosses]
        extras = [dot(circ[s], edge) for s, (_, edge) in pairs]
        corrs = []
        for inner, extra in zip(inners, extras):
            inner_re = inner[:HALF].astype(BF16)
            inner_im = (inner[HALF:] + extra).astype(BF16)
            stacked = [
                jnp.concatenate([inner_re[:, lanes], inner_im[:, lanes]], axis=1)
                for lanes in (slice(0, HALF), slice(HALF, EDGE))
            ]
            corrs.append(dot(jnp.concatenate(stacked, axis=0), back_rows[...]))
        for (s, _), corr in zip(pairs, corrs):
            one, two = corr[:HALF], corr[HALF:]
            stats[s, 0] = jnp.maximum(stats[s, 0], jnp.maximum(one, two))
            stats[s, 1] = stats[s, 1] + (one + two)
            stats[s, 2] = stats[s, 2] + (one * one + two * two)

    arrive(slot(1 - core, 0))
    arrive(slot(0, 1))
    arrive(slot(1, 1))
    now, spare = spectra((0, 1))
    correlate([(0, now), (1, now)])

    def chip_before():
        for block in (3, 2):
            for at in range(2):
                arrive(slot(block, at))
        one, two = spectra((3, 2))
        correlate([(1, one), (1, two)])
        correlate([(0, one), (0, two)])

    def two_before():
        @pl.when(odd == 0)
        def _():
            arrive(slot(4, 0))

        arrive(slot(4, 1))
        (far,) = spectra((4,))
        guest = [jnp.where(is_guest, f.astype(F32), c.astype(F32)).astype(BF16) for f, c in zip(far, held())]
        correlate([(0, far), (1, guest)])

    held_proj[...], held_edge[...] = spare

    def held():
        return held_proj[...], held_edge[...]

    each_variant(pass_near, first_plane)
    sent.update(after)

    def last_steps(step, carry):
        pl.when((step == 0) == (odd == 1))(chip_before)
        pl.when((step == 0) == (odd == 0))(two_before)
        return carry

    lax.fori_loop(0, 2, last_steps, 0)

    theirs = [
        copy_of(parts.at[s], taken_out.at[s], part_send.at[s], part_recv.at[s], sibling)
        for s in range(2)
    ]
    ours = [pltpu.make_async_copy(parts.at[s], own_out.at[s], load_sem.at[s]) for s in range(2)]
    parts[1] = stats[1].astype(BF16)
    theirs[1].start()
    parts[0] = stats[0].astype(BF16)

    @pl.when(core == 1)
    def _():
        theirs[0].start()

    @pl.when(core == 0)
    def _():
        ours[0].start()

    ours[1].start()
    each_variant(finish)
    for copy in tile_copies:
        copy.wait_send()
    theirs[1].wait()
    ours[1].wait()

    @pl.when(core == 1)
    def _():
        theirs[0].wait_send()

    @pl.when(core == 0)
    def _():
        theirs[0].wait_recv()
        ours[0].wait()


def merge_kernel(counts, own, taken, peak_out, score_out):
    me = lax.axis_index("blk")
    is_first = me % 2 == 0
    live = counts[me]
    peaks, scores = [], []
    for s in range(2):
        mine, theirs = own[s].astype(F32), taken[s].astype(F32)
        peak = jnp.maximum(mine[0], theirs[0])
        mean = (mine[1] + theirs[1]) * (1.0 / 16)
        square = (mine[2] + theirs[2]) * (1.0 / 16)
        variance = jnp.maximum(square - mean * mean, 0.3)
        peaks.append(peak)
        scores.append((peak - mean) * lax.rsqrt(variance))
    for out, maps in ((peak_out, peaks), (score_out, scores)):
        out[0] = jnp.where(live > 0, jnp.where(is_first, maps[0], maps[1]), 0.0)
        out[1] = jnp.where(live > 1, maps[1], 0.0)


def body(tile_pool, tile_list, counts, projections):
    tables = [jnp.asarray(t) for t in make_tables()]
    any_spec = pl.BlockSpec(memory_space=pl.ANY)
    vmem = pl.BlockSpec(memory_space=pltpu.VMEM)
    smem = pl.BlockSpec(memory_space=pltpu.SMEM)
    own, taken = pl.pallas_call(
        kernel,
        out_shape=(
            jax.ShapeDtypeStruct((2, 3, HALF, EDGE), BF16),
            jax.ShapeDtypeStruct((2, 3, HALF, EDGE), BF16),
        ),
        in_specs=[any_spec, smem, smem] + [any_spec] * 8,
        out_specs=(any_spec, any_spec),
        scratch_shapes=[
            pltpu.VMEM((4, EDGE, EDGE), BF16),
            pltpu.VMEM((2, SIDE, SIDE), BF16),
            pltpu.VMEM((3, EDGE, EDGE), BF16),
            pltpu.VMEM((2 * EDGE, 2 * EDGE), BF16),
            pltpu.VMEM((2 * EDGE, 2 * SIDE), BF16),
            pltpu.VMEM((EDGE, 2 * EDGE), BF16),
            pltpu.VMEM((EDGE, EDGE), BF16),
            pltpu.VMEM((16, EDGE), BF16),
            pltpu.VMEM((HALF, HALF), BF16),
            pltpu.VMEM((2,) + UNIT, BF16),
            pltpu.VMEM((STAGE + 1,) + UNIT, BF16),
            pltpu.VMEM((2, EDGE, EDGE), BF16),
            pltpu.VMEM((2, EDGE, EDGE), BF16),
            pltpu.VMEM((2, 2 * EDGE, EDGE), BF16),
            pltpu.VMEM((2, HALF, SIDE), BF16),
            pltpu.VMEM((2, 3, HALF, EDGE), F32),
            pltpu.VMEM((2 * EDGE, EDGE), BF16),
            pltpu.VMEM((SIDE, EDGE), BF16),
            pltpu.VMEM((2, 3, HALF, EDGE), BF16),
            pltpu.SemaphoreType.DMA((9,)),
            pltpu.SemaphoreType.DMA((32,)),
            pltpu.SemaphoreType.DMA((STAGE + 1,)),
            pltpu.SemaphoreType.DMA((2 * PIECES,)),
            pltpu.SemaphoreType.DMA((2,)),
            pltpu.SemaphoreType.DMA((2,)),
            pltpu.SemaphoreType.DMA((2,)),
            pltpu.SemaphoreType.DMA((2,)),
        ],
        compiler_params=pltpu.CompilerParams(
            collective_id=0, has_side_effects=True, vmem_limit_bytes=56 << 20
        ),
    )(tile_pool, tile_list, counts, projections, *tables)
    out = jax.ShapeDtypeStruct((2, HALF, EDGE), F32)
    part = pl.BlockSpec((2, 3, HALF // 2, EDGE), lambda i: (0, 0, i, 0))
    out_part = pl.BlockSpec((2, HALF // 2, EDGE), lambda i: (0, i, 0))
    return pl.pallas_call(
        merge_kernel,
        grid=(2,),
        out_shape=(out, out),
        in_specs=[smem, part, part],
        out_specs=(out_part, out_part),
    )(counts, own, taken)


def solution(mesh):
    in_specs = (P("blk", None, None), P("blk"), P(), P(("blk", "bank"), None, None))
    out_specs = (P("blk", "bank", None), P("blk", "bank", None))
    return jax.shard_map(body, mesh=mesh, in_specs=in_specs, out_specs=out_specs, check_vma=False)
```
